512 devices in a mesh: seg: 16 (over x, y), op: 32 (over z, core).
Axes of the slice: x: 4, y: 4, z: 16, core: 2. Of those that a mesh axis runs over, the one named last changes fastest.
Arguments:
- theta: bfloat16 [16, 32, 512, 512], P('seg', 'op'), may hold values from -21 to 21
- left_edge: bfloat16 [32, 512, 512], P('op'), may hold values from -1 to 4
- transfer: bfloat16 [16, 32, 512, 512], P('seg', 'op'), may hold values from -1 to 2
- right_env: bfloat16 [16, 32, 512, 512], P('seg', 'op'), may hold values from -1 to 4
- coupling: bfloat16 [16, 32, 512, 512], P('seg', 'op'), may hold values from -0.25 to 0.25
- left_sizes: int32 [32], P('op'), may hold values from 1 to 512, 12288 in all
- right_sizes: int32 [32], P('op'), may hold values from 1 to 512, 12288 in all
Outputs:
- theta_out: float32 [16, 32, 512, 512], P('seg', 'op')
- left_env: bfloat16 [16, 32, 512, 512], P('seg', 'op')
- energy: float32 [16], P('seg')
- first_energy: float32 [16], P('seg')
The draws below stay inside these ranges and needn't reach their ends.
All inputs are finite; a program needn't handle non-finite values. No bound on the sum of `left_sizes` or of `right_sizes` on one device may be relied on, other than what follows from the above.
Results may differ from the reference program's by a relative error of at most 0.0085.
Values may be sent and summed in bfloat16 or wider, within the bound.
No kernel may reach another device: no remote copies, remote signals or barrier semaphores. Data moves between devices by JAX's collectives and lax.ppermute only.
A program may use at most 128 MiB of HBM per device.

```python
import math
import jax
import jax.numpy as jnp
import numpy as np
from jax import lax

BLK = 512
DAVIDSON = 4
SECTORS = 32
SEGMENTS = 16


def scaled_noise(key, shape):
    noise = jnp.clip(jax.random.normal(key, shape, jnp.float32), -4.0, 4.0)
    return noise / jnp.sqrt(jnp.float32(BLK))


def draw_transfer(key, part):
    shape = (SEGMENTS, SECTORS, BLK, BLK)
    noise = scaled_noise(jax.random.fold_in(key, 11), shape)
    identity = jnp.eye(BLK, dtype=jnp.float32)
    return (identity + 0.25 * noise).astype(jnp.bfloat16)


def draw_left_edge(key, part):
    shape = (SECTORS, BLK, BLK)
    noise = scaled_noise(jax.random.fold_in(key, 23), shape)
    level = jax.random.uniform(jax.random.fold_in(key, 29), (SECTORS,), jnp.float32, 0.5, 1.5)
    identity = jnp.eye(BLK, dtype=jnp.float32)
    return (identity[None] * level[:, None, None] + noise).astype(jnp.bfloat16)


def draw_right_env(key, part):
    shape = (SEGMENTS, SECTORS, BLK, BLK)
    noise = scaled_noise(jax.random.fold_in(key, 37), shape)
    log_level = jax.random.uniform(jax.random.fold_in(key, 41), (SEGMENTS,), jnp.float32, jnp.log(0.5), jnp.log(2.0))
    sector_level = jax.random.uniform(jax.random.fold_in(key, 43), (SEGMENTS, SECTORS), jnp.float32, 0.75, 1.25)
    level = jnp.exp(log_level)[:, None] * sector_level
    identity = jnp.eye(BLK, dtype=jnp.float32)
    return (identity[None, None] * level[:, :, None, None] + noise).astype(jnp.bfloat16)


def draw_theta(key, part):
    shape = (SEGMENTS, SECTORS, BLK, BLK)
    subkey = jax.random.fold_in(key, 53)
    position = jnp.arange(SECTORS, dtype=jnp.float32) / jnp.float32(SECTORS - 1)
    noise = jnp.clip(jax.random.normal(subkey, shape, jnp.float32), -4.0, 4.0)
    level = jnp.exp(jnp.log(5.0) * position)
    return (noise * level[None, :, None, None]).astype(jnp.bfloat16)


def levels(stream_key, dims, shards, least, top_value):
    factor_of, own = 1.0, jax.random.fold_in(stream_key, 6)
    for dim, blocks in shards:
        draws = jnp.exp(jax.random.uniform(jax.random.fold_in(own, dim), (blocks,), jnp.float32, least / len(shards), top_value / len(shards)))
        factor_of = factor_of * jnp.repeat(draws, dims[dim] // blocks).reshape([-1 if axis == dim else 1 for axis in range(len(dims))])
    return factor_of


def length_profile(amount, total, bound, slope):
    weights = [(1 << 20) // math.isqrt(grade ** slope) + 1 for grade in range(2, amount + 1)]
    rest, holding = total - bound - (amount - 1), [1] * (amount - 1)
    while rest > 0:
        movable = [i for i in range(amount - 1) if holding[i] < bound]
        whole, left = sum([weights[i] for i in movable]), rest
        for i in movable:
            more = min(bound - holding[i], max(1, left * weights[i] // whole), rest)
            holding[i] = holding[i] + more
            rest = rest - more
    return np.array([bound] + holding)


def ragged(own_key, amount, total, most, lean):
    if amount == 2:
        one = jax.random.randint(own_key, (), max(1, total - most), min(most, total - 1) + 1)
        return jnp.stack([one, total - one])
    tallies = jnp.asarray(length_profile(amount, total, most, lean), jnp.int32)
    couples = (amount - 1) // 2
    giver, receiver = tallies[1:1 + 2 * couples:2], tallies[2:2 + 2 * couples:2]
    room = jnp.minimum(giver - 1, most - receiver)
    passed = jax.random.randint(jax.random.fold_in(own_key, 1), (couples,), 0, 1 << 20) % (room + 1)
    tallies = tallies.at[1:1 + 2 * couples:2].set(giver - passed).at[2:2 + 2 * couples:2].set(receiver + passed)
    return tallies[jax.random.permutation(jax.random.fold_in(own_key, 2), amount)]


def bell_draw(stream_key, shape, scale, most, cuts=(), kind=jnp.bfloat16):
    values = jax.random.normal(stream_key, shape, jnp.float32) * scale
    if len(cuts) > 0:
        values = levels(stream_key, shape, cuts, -0.22, 0.18) * values
    return jnp.clip(values, min=-most, max=most).astype(kind)


def setup_inputs(seed: int = 0) -> dict:
    key_list = jax.random.split(jax.random.key(seed), 8)
    return {
        "theta": draw_theta(jax.random.fold_in(key_list[7], 71), 0),
        "left_edge": draw_left_edge(jax.random.fold_in(key_list[7], 71), 0),
        "transfer": draw_transfer(jax.random.fold_in(key_list[7], 71), 0),
        "right_env": draw_right_env(jax.random.fold_in(key_list[7], 71), 0),
        "coupling": bell_draw(key_list[4], (SEGMENTS, SECTORS, BLK, BLK), BLK ** -0.5, 0.25, ((0, 16), (1, 32))),
        "left_sizes": ragged(key_list[5], SECTORS, SECTORS * BLK * 3 // 4, BLK, 1).astype(jnp.int32),
        "right_sizes": ragged(key_list[6], SECTORS, SECTORS * BLK * 3 // 4, BLK, 1).astype(jnp.int32),
    }


epsilon = 1e-06

def symmetric(block):
    return 0.5 * (block + jnp.swapaxes(block, -1, -2))

def apply_all(field, left_block, right_block, coupling_blk, live_mask):
    field_wide = field.astype(jnp.float32)
    middle = jnp.einsum('kij,kjl->kil', left_block.astype(jnp.float32), field_wide).astype(jnp.bfloat16)
    diagonal_term = jnp.einsum('kij,kjl->kil', middle.astype(jnp.float32), right_block.astype(jnp.float32))
    coupling_wide = coupling_blk.astype(jnp.float32)
    previous = jnp.concatenate([jnp.zeros_like(field_wide[:1]), field_wide[:-1]], 0)
    lower_term = jnp.einsum('kij,kjl->kil', coupling_wide, previous)
    lifted = jnp.einsum('kji,kjl->kil', coupling_wide, field_wide)
    upper_part = jnp.concatenate([lifted[1:], jnp.zeros_like(lifted[:1])], 0)
    return live_mask * (diagonal_term + lower_term + upper_part)

def reference(theta, left_edge, transfer, right_env, coupling, left_sizes, right_sizes):
    row_index = lax.broadcasted_iota(jnp.int32, (SECTORS, BLK, BLK), 1)
    col_index = lax.broadcasted_iota(jnp.int32, (SECTORS, BLK, BLK), 2)
    live_mask = ((row_index < left_sizes[:, None, None]) & (col_index < right_sizes[:, None, None])).astype(jnp.float32)
    edge_sym = symmetric(left_edge.astype(jnp.float32))
    identity = jnp.broadcast_to(jnp.eye(BLK, dtype=jnp.float32), (SECTORS, BLK, BLK))
    highest = lax.Precision.HIGHEST

    def segment_solve(prefix, pieces):
        start_blk, step_blk, right_raw, coupling_blk = pieces
        left_block = jnp.einsum('kji,kjl->kil', prefix, edge_sym, precision=highest)
        left_block = jnp.einsum('kij,kjl->kil', left_block, prefix, precision=highest).astype(jnp.bfloat16)
        right_block = symmetric(right_raw.astype(jnp.float32)).astype(jnp.bfloat16)
        start = live_mask * start_blk.astype(jnp.float32)
        vector = start / jnp.sqrt(jnp.sum(start * start) + epsilon)
        image = apply_all(vector.astype(jnp.bfloat16), left_block, right_block, coupling_blk, live_mask)
        energy = jnp.sum(vector * image)
        first_value = energy
        for sweep_step in range(DAVIDSON):
            residual = image - energy * vector
            correction = residual.astype(jnp.bfloat16)
            corr_wide = correction.astype(jnp.float32)
            applied = apply_all(correction, left_block, right_block, coupling_blk, live_mask)
            corr_norm = jnp.sum(corr_wide * corr_wide)
            cross_term = jnp.sum(image * corr_wide)
            curv_term = jnp.sum(corr_wide * applied)
            scale_norm = jnp.sqrt(corr_norm + epsilon)
            offdiag = cross_term / scale_norm
            diag_value = curv_term / (corr_norm + epsilon)
            half_gap = (diag_value - energy) / 2
            lowest = (energy + diag_value) / 2 - jnp.sqrt(half_gap * half_gap + offdiag * offdiag)
            rotation = lowest - energy
            radius = jnp.sqrt(offdiag * offdiag + rotation * rotation + epsilon)
            vector = (offdiag * vector + rotation * corr_wide / scale_norm) / radius
            image = (offdiag * image + rotation * applied / scale_norm) / radius
            energy = lowest
        prefix_next = jnp.einsum('kij,kjl->kil', prefix, step_blk.astype(jnp.float32), precision=highest)
        return (prefix_next, (vector, left_block, energy, first_value))
    final_prefix, outputs = lax.scan(segment_solve, identity, (theta, transfer, right_env, coupling))
    return (outputs[0], outputs[1], outputs[2], outputs[3])
```

```python
import functools

import jax
import jax.numpy as jnp
from jax import lax
from jax.experimental import pallas as pl
from jax.experimental.pallas import tpu as pltpu
from jax.sharding import PartitionSpec as P

DAVIDSON = 4
ROW = 4
LANES = 128
STEP = 128
BAND = 32
SHIFT = 2.0
epsilon = 1e-06

f32, bf16 = jnp.float32, jnp.bfloat16
VMEM = pl.BlockSpec(memory_space=pltpu.VMEM)
SMEM = pl.BlockSpec(memory_space=pltpu.SMEM)


def wide_dot(a, b):
    return jnp.dot(a, b, preferred_element_type=f32)


def left_transposed_dot(a, b):
    return lax.dot_general(a, b, (((0,), (0,)), ((), ())), preferred_element_type=f32)


def split(x):
    high = x.astype(bf16)
    return high, (x - high.astype(f32)).astype(bf16)


def total(x):
    return jnp.sum(jnp.sum(x, axis=0, keepdims=True), axis=1, keepdims=True)


def in_lanes(first, values):
    lane = lax.broadcasted_iota(jnp.int32, (1, LANES), 1)
    out = jnp.zeros((1, LANES), f32)
    for i, value in enumerate(values):
        out = jnp.where(lane == first + i, value, out)
    return out


def live(start, rows, cols, sizes):
    row = lax.broadcasted_iota(jnp.int32, (rows, cols), 0) + start
    col = lax.broadcasted_iota(jnp.int32, (rows, cols), 1)
    return (row < sizes[0]) & (col < sizes[1])


def banded_dots(fields, last):
    n, cols = last.shape

    def band(i, sums):
        at = pl.ds(pl.multiple_of(i * BAND, BAND), BAND)
        mine = last[at, :].astype(f32)
        return tuple(
            s + jnp.sum((f[at, :].astype(f32) * mine).reshape(BAND // 8, 8, cols), axis=0)
            for s, f in zip(sums, fields, strict=True)
        )

    sums = lax.fori_loop(0, n // BAND, band, tuple(jnp.zeros((8, cols), f32) for _ in fields))
    return [total(s) for s in sums]


def call(kernel, out, flops=2e8, bytes_accessed=3e6, smem=1, scratch=()):
    def run(*args):
        return pl.pallas_call(
            kernel,
            out_shape=out,
            in_specs=[SMEM] * smem + [VMEM] * (len(args) - smem),
            out_specs=jax.tree.map(lambda _: VMEM, out),
            scratch_shapes=list(scratch),
            cost_estimate=pl.CostEstimate(
                flops=int(flops), bytes_accessed=int(bytes_accessed), transcendentals=0
            ),
            compiler_params=pltpu.CompilerParams(vmem_limit_bytes=48 * 1024 * 1024),
        )(*args)

    return run


def prepare_kernel(sizes, theta, edge, right, field, edge_out, right_out, lifted, stats):
    n = theta.shape[0]
    for c in range(0, n, STEP):
        keep = live(c, STEP, n, sizes)
        field[c : c + STEP, :] = jnp.where(
            keep, theta[c : c + STEP, :].astype(f32), 0.0
        ).astype(bf16)
    for source, out in ((edge, edge_out), (right, right_out)):
        for c in range(0, n, STEP):
            turned = source[:, c : c + STEP].astype(f32).T
            out[c : c + STEP, :] = (0.5 * (source[c : c + STEP, :].astype(f32) + turned)).astype(
                out.dtype
            )
    for c in range(0, n, STEP):
        lifted[c : c + STEP, :] = wide_dot(field[c : c + STEP, :], right_out[...]).astype(bf16)
    stats[...] = in_lanes(0, banded_dots([field], field))


def survey_kernel(transfer, edge, right, coupling, stats):
    n = transfer.shape[0]
    (grown,), (edge_sq,), (right_sq,), (coupling_sq,) = (
        banded_dots([x], x) for x in (transfer, edge, right, coupling)
    )
    edge_trace = right_trace = jnp.zeros((1, 1), f32)
    for c in range(0, n, LANES):
        diagonal = lax.broadcasted_iota(jnp.int32, (LANES, LANES), 0) == lax.broadcasted_iota(
            jnp.int32, (LANES, LANES), 1
        )
        at = slice(c, c + LANES)
        edge_trace += total(jnp.where(diagonal, edge[at, at].astype(f32), 0.0))
        right_trace += total(jnp.where(diagonal, right[at, at].astype(f32), 0.0))
    values = (
        grown / n,
        jnp.sqrt(edge_sq / n) * jnp.sqrt(right_sq / n),
        coupling_sq / n,
        edge_trace / n * (right_trace / n),
    )
    stats[...] = jnp.broadcast_to(in_lanes(0, values), stats.shape)


def couple_kernel(place, coupling, above, field_a, field_b, near, far, image):
    n = coupling.shape[0]
    odd = place[0] == 1

    @pl.when(odd)
    def _():
        near[...] = coupling[...]
        for c in range(0, n, STEP):
            far[c : c + STEP, :] = above[:, c : c + STEP].astype(f32).T.astype(bf16)

    @pl.when(jnp.logical_not(odd))
    def _():
        far[...] = coupling[...]
        for c in range(0, n, STEP):
            near[c : c + STEP, :] = above[:, c : c + STEP].astype(f32).T.astype(bf16)

    for c in range(0, n, STEP):
        at = slice(c, c + STEP)
        image[at, :] = wide_dot(near[at, :], field_a[...]) + wide_dot(far[at, :], field_b[...])


def in_order(place, own, behind, ahead, across, held):
    held[place] = own[...]
    held[lax.rem(place + 1, ROW)] = ahead[...]
    held[lax.rem(place + 2, ROW)] = across[...]
    held[lax.rem(place + 3, ROW)] = behind[...]


def row_kernel(place, own, behind, ahead, across, whole, high, low, held):
    y = place[0]
    in_order(y, own, behind, ahead, across, held)
    n = own.shape[0]

    @pl.when(y == 0)
    def _():
        row = lax.broadcasted_iota(jnp.int32, (n, n), 0)
        col = lax.broadcasted_iota(jnp.int32, (n, n), 1)
        high[...] = jnp.where(row == col, 1.0, 0.0).astype(bf16)
        low[...] = jnp.zeros((n, n), bf16)

    @pl.when(y == 1)
    def _():
        high[...] = held[0]
        low[...] = jnp.zeros((n, n), bf16)

    product = wide_dot(held[0], held[1])
    for position in range(2, ROW):
        upper, lower = split(product)

        @pl.when(y == position)
        def _(upper=upper, lower=lower):
            high[...] = upper
            low[...] = lower

        product = wide_dot(upper, held[position]) + wide_dot(lower, held[position])
    whole[...] = product.astype(bf16)


def segment_kernel(
    place, tune, own, behind, ahead, across, high_in, low_in, edge, lifted, couplings, field,
    left, next_field, held, high, low,
):
    x = place[0]
    sizes = (place[1], place[2])
    n = own.shape[0]
    in_order(x, own, behind, ahead, across, held)
    high[...] = high_in[...]
    low[...] = low_in[...]
    for position in range(ROW - 2, -1, -1):

        @pl.when(position < x)
        def _(position=position):
            product = wide_dot(held[position], high[...]) + wide_dot(held[position], low[...])
            upper, lower = split(product)
            high[...] = upper
            low[...] = lower

    edge_high, edge_low = split(edge[...])
    turned = (
        wide_dot(edge_high, high[...]) + wide_dot(edge_high, low[...]) + wide_dot(edge_low, high[...])
    )
    upper, lower = split(turned)
    block = (
        left_transposed_dot(high[...], upper)
        + left_transposed_dot(low[...], upper)
        + left_transposed_dot(high[...], lower)
    ).astype(bf16)
    left[...] = block
    for c in range(0, n, STEP):
        at = slice(c, c + STEP)
        image = wide_dot(left[at, :], lifted[...]) + couplings[at, :]
        moved = (image - tune[0] * field[at, :].astype(f32)) * tune[1]
        next_field[at, :] = jnp.where(live(c, STEP, n, sizes), moved, 0.0).astype(bf16)


def local_kernel(count, left, right, near, field_a, *rest):
    fields, (partial, stats) = rest[:count], rest[count:]
    field = fields[-1]
    n = field.shape[0]
    for c in range(0, n, STEP):
        at = slice(c, c + STEP)
        middle = wide_dot(left[at, :], field[...]).astype(bf16)
        partial[at, :] = wide_dot(middle, right[...]) + wide_dot(near[at, :], field_a[...])
    k = count - 1
    stats[...] = in_lanes(k * (k + 1) // 2, banded_dots(list(fields), field))


def advance_kernel(place, tune, partial, far, field_b, field, next_field):
    sizes = (place[1], place[2])
    n = field.shape[0]
    for c in range(0, n, STEP):
        at = slice(c, c + STEP)
        image = partial[at, :] + wide_dot(far[at, :], field_b[...])
        moved = (image - tune[0] * field[at, :].astype(f32)) * tune[1]
        next_field[at, :] = jnp.where(live(c, STEP, n, sizes), moved, 0.0).astype(bf16)


def advance_last_kernel(place, tune, partial, far, field_b, field, next_field, sent, kept):
    advance_kernel(place, tune, partial, far, field_b, field, next_field)
    half = field.shape[1] // 2

    @pl.when(place[0] == 1)
    def _():
        sent[...] = next_field[:, :half]
        kept[...] = next_field[:, half:]

    @pl.when(place[0] != 1)
    def _():
        sent[...] = next_field[:, half:]
        kept[...] = next_field[:, :half]


def close_kernel(count, far, got, kept, partial, last, *rest):
    stats_in, out = rest[:count], rest[count]
    n = last.shape[0]
    inner = jnp.zeros((1, 1), f32)
    for c in range(0, n, STEP):
        at = slice(c, c + STEP)
        crossing = wide_dot(far[at, :], got[...]) * kept[at, :].astype(f32)
        inner += 2.0 * total(crossing) + total(partial[at, :] * last[at, :].astype(f32))
    k = DAVIDSON + 1
    sums = in_lanes(k * (k + 1) // 2, [inner])
    for piece in stats_in:
        sums += piece[...]
    out[...] = jnp.broadcast_to(sums, out.shape)


def solve_kernel(tune, sums, *rest):
    size = DAVIDSON + 1
    fields, (vector, energies) = rest[:size], rest[size:]
    shift = jnp.full((1, 1), tune[0], f32)
    scale = jnp.full((1, 1), tune[2], f32)
    row = jnp.sum(sums[...], axis=0, keepdims=True)
    lane = lax.broadcasted_iota(jnp.int32, (1, LANES), 1)

    def entry(i):
        return jnp.sum(jnp.where(lane == i, row, 0.0), axis=1, keepdims=True)

    gram = {}
    for k in range(size):
        for j in range(k + 1):
            gram[j, k] = gram[k, j] = entry(k * (k + 1) // 2 + j)
    image_gram = {}
    for j in range(size):
        for k in range(j, size):
            if j < size - 1:
                value = scale * gram[j + 1, k] + shift * gram[j, k]
            else:
                value = entry(size * (size + 1) // 2)
            image_gram[j, k] = image_gram[k, j] = value

    def form(table, a, b):
        out = jnp.zeros((1, 1), f32)
        for j, aj in enumerate(a):
            if aj is None:
                continue
            inner = jnp.zeros((1, 1), f32)
            for k, bk in enumerate(b):
                if bk is not None:
                    inner = inner + table[j, k] * bk
            out = out + aj * inner
        return out

    weights = [1.0 / jnp.sqrt(gram[0, 0] + epsilon)] + [None] * (size - 1)
    energy = first = form(image_gram, weights, weights)
    for step in range(DAVIDSON):
        turn = [None] * size
        for k in range(step + 2):
            value = None
            if weights[k] is not None:
                value = (shift - energy) * weights[k]
            if k > 0 and weights[k - 1] is not None:
                carried = scale * weights[k - 1]
                value = carried if value is None else value + carried
            turn[k] = value
        corr_norm = jnp.maximum(form(gram, turn, turn), 0.0)
        cross_term = form(image_gram, weights, turn)
        curv_term = form(image_gram, turn, turn)
        scale_norm = jnp.sqrt(corr_norm + epsilon)
        offdiag = cross_term / scale_norm
        diag_value = curv_term / (corr_norm + epsilon)
        half_gap = (diag_value - energy) / 2
        lowest = (energy + diag_value) / 2 - jnp.sqrt(half_gap * half_gap + offdiag * offdiag)
        rotation = lowest - energy
        radius = jnp.sqrt(offdiag * offdiag + rotation * rotation + epsilon)
        keep, add = offdiag / radius, rotation / scale_norm / radius
        weights = [
            None
            if t is None
            else add * t if w is None else keep * w + add * t
            for w, t in zip(weights, turn, strict=True)
        ]
        energy = lowest
    energies[...] = in_lanes(0, [energy, first])
    n = vector.shape[0]

    def band(i, carry):
        at = pl.ds(pl.multiple_of(i * BAND, BAND), BAND)
        out = weights[0] * fields[0][at, :].astype(f32)
        for w, field in zip(weights[1:], fields[1:], strict=True):
            out = out + w * field[at, :].astype(f32)
        vector[at, :] = out
        return carry

    lax.fori_loop(0, n // BAND, band, 0)


def routes(axis_size):
    def along_y(d):
        return [(s, s - s % ROW + (s + d) % ROW) for s in range(axis_size)]

    def along_x(d):
        return [(s, (s + ROW * d) % axis_size) for s in range(axis_size)]

    return along_y, along_x


def on_device(theta, left_edge, transfer, right_env, coupling, left_sizes, right_sizes):
    n = theta.shape[-1]
    theta, left_edge = theta[0, 0], left_edge[0]
    transfer, right_env, coupling = transfer[0, 0], right_env[0, 0], coupling[0, 0]
    seg, op = lax.axis_index("seg"), lax.axis_index("op")
    segments, sectors = lax.axis_size("seg"), lax.axis_size("op")
    along_y, along_x = routes(segments)
    near_swap = [(i, i ^ 1) for i in range(sectors)]
    far_swap = [(i, i + 1 if i % 2 else i - 1) for i in range(1, sectors - 1)]
    down = [(i + 1, i) for i in range(sectors - 1)]
    square, wide = jax.ShapeDtypeStruct((n, n), bf16), jax.ShapeDtypeStruct((n, n), f32)
    tall = jax.ShapeDtypeStruct((n, n // 2), bf16)
    lanes = jax.ShapeDtypeStruct((1, LANES), f32)
    spread = jax.ShapeDtypeStruct((sectors, LANES), f32)
    sizes = jnp.concatenate([left_sizes, right_sizes])
    odd = lax.rem(op, 2)
    place = jnp.concatenate([jnp.reshape(odd, (1,)), sizes])

    def seg_send(x, route):
        return lax.ppermute(x, "seg", route)

    def op_send(x, route):
        return lax.ppermute(x, "op", route)

    def op_sum(x):
        return lax.all_to_all(x[:, None], "op", 0, 0)[:, 0]

    t_behind = seg_send(transfer, along_y(1))
    t_ahead = seg_send(transfer, along_y(-1))
    t_across = seg_send(transfer, along_y(2))

    field, edge_sym, right, lifted, stats = call(
        prepare_kernel, (square, wide, square, square, lanes)
    )(sizes, theta, left_edge, right_env)
    above = op_send(coupling, down)
    field_b = op_send(field, far_swap)
    field_a = op_send(field, near_swap)
    near, far, couplings = call(couple_kernel, (square, square, wide))(
        place, coupling, above, field_a, field_b
    )
    survey = call(survey_kernel, spread, smem=0)(transfer, left_edge, right_env, coupling)

    whole, high, low = call(
        row_kernel,
        (square, square, square),
        scratch=[pltpu.VMEM((ROW, n, n), bf16)],
    )(jnp.reshape(lax.rem(seg, ROW), (1,)), transfer, t_behind, t_ahead, t_across)
    r_behind = seg_send(whole, along_x(1))
    r_ahead = seg_send(whole, along_x(-1))
    r_across = seg_send(whole, along_x(2))

    found = jnp.sum(op_sum(survey), axis=0) / sectors
    growth = jnp.exp(
        jnp.clip(seg.astype(f32) * jnp.log(jnp.maximum(found[0], 1e-30)), -30.0, 30.0)
    )
    scale = found[1] * growth + 2.0 * jnp.sqrt(found[2]) + 1e-12
    shift = SHIFT * found[3] * growth
    tune = jnp.stack([shift, 1.0 / scale, scale])

    left, following = call(
        segment_kernel,
        (square, square),
        smem=2,
        scratch=[
            pltpu.VMEM((ROW, n, n), bf16),
            pltpu.VMEM((n, n), bf16),
            pltpu.VMEM((n, n), bf16),
        ],
    )(
        jnp.concatenate([jnp.reshape(seg // ROW, (1,)), sizes]), tune,
        whole, r_behind, r_ahead, r_across, high, low, edge_sym, lifted, couplings, field,
    )
    fields, pieces = [field, following], [stats]
    sent = kept = None
    for k in range(1, DAVIDSON + 1):
        last = k == DAVIDSON
        newest = fields[-1]
        field_b = op_send(sent if last else newest, far_swap)
        field_a = op_send(newest, near_swap)
        partial, stats = call(functools.partial(local_kernel, k + 1), (wide, lanes), smem=0)(
            left, right, near, field_a, *fields
        )
        pieces.append(stats)
        if last:
            sums = call(functools.partial(close_kernel, len(pieces)), spread, smem=0)(
                far, field_b, kept, partial, newest, *pieces
            )
        elif k == DAVIDSON - 1:
            following, sent, kept = call(advance_last_kernel, (square, tall, tall), smem=2)(
                place, tune, partial, far, field_b, newest
            )
            fields.append(following)
        else:
            following = call(advance_kernel, square, smem=2)(
                place, tune, partial, far, field_b, newest
            )
            fields.append(following)
    vector, energies = call(solve_kernel, (wide, lanes))(tune, op_sum(sums), *fields)
    return (
        vector[None, None],
        left[None, None],
        energies[0, 0:1],
        energies[0, 1:2],
    )


def solution(mesh):
    placed = (
        P("seg", "op", None, None),
        P("op", None, None),
        P("seg", "op", None, None),
        P("seg", "op", None, None),
        P("seg", "op", None, None),
        P("op"),
        P("op"),
    )
    return jax.shard_map(
        on_device,
        mesh=mesh,
        in_specs=placed,
        out_specs=(P("seg", "op", None, None), P("seg", "op", None, None), P("seg"), P("seg")),
        check_vma=False,
    )
```

```python
import functools

import jax
import jax.numpy as jnp
from jax import lax
from jax.experimental import pallas as pl
from jax.experimental.pallas import tpu as pltpu
from jax.sharding import PartitionSpec as P

DAVIDSON = 4
ROW = 4
LANES = 128
STEP = 256
BAND = 32
SHIFT = 2.0
GRANT = 52
epsilon = 1e-06

f32, bf16 = jnp.float32, jnp.bfloat16
VMEM = pl.BlockSpec(memory_space=pltpu.VMEM)
SMEM = pl.BlockSpec(memory_space=pltpu.SMEM)
LOOSE = pl.BlockSpec(memory_space=pl.ANY)
HBM = pl.BlockSpec(memory_space=pltpu.HBM)
DMA = pltpu.SemaphoreType.DMA


def wide_dot(a, b):
    return jnp.dot(a, b, preferred_element_type=f32)


def left_transposed_dot(a, b):
    return lax.dot_general(a, b, (((0,), (0,)), ((), ())), preferred_element_type=f32)


def split(x):
    high = x.astype(bf16)
    return high, (x - high.astype(f32)).astype(bf16)


def total(x):
    return jnp.sum(jnp.sum(x, axis=0, keepdims=True), axis=1, keepdims=True)


def in_lanes(first, values):
    lane = lax.broadcasted_iota(jnp.int32, (1, LANES), 1)
    out = jnp.zeros((1, LANES), f32)
    for i, value in enumerate(values):
        out = jnp.where(lane == first + i, value, out)
    return out


def live(start, rows, cols, sizes):
    row = lax.broadcasted_iota(jnp.int32, (rows, cols), 0) + start
    col = lax.broadcasted_iota(jnp.int32, (rows, cols), 1)
    return (row < sizes[0]) & (col < sizes[1])


def banded_dots(fields, last):
    n, cols = last.shape

    def band(i, sums):
        at = pl.ds(pl.multiple_of(i * BAND, BAND), BAND)
        mine = last[at, :].astype(f32)
        return tuple(
            s + jnp.sum((f[at, :].astype(f32) * mine).reshape(BAND // 8, 8, cols), axis=0)
            for s, f in zip(sums, fields, strict=True)
        )

    sums = lax.fori_loop(0, n // BAND, band, tuple(jnp.zeros((8, cols), f32) for _ in fields))
    return [total(s) for s in sums]


def call(kernel, out, smem=1, loose=0, far=0, scratch=(), out_specs=None, grant=20):
    def run(*args):
        return pl.pallas_call(
            kernel,
            out_shape=out,
            in_specs=[SMEM] * smem
            + [VMEM] * (len(args) - smem - loose - far)
            + [LOOSE] * loose
            + [HBM] * far,
            out_specs=jax.tree.map(lambda _: VMEM, out) if out_specs is None else out_specs,
            scratch_shapes=list(scratch),
            cost_estimate=pl.CostEstimate(
                flops=1, bytes_accessed=1, transcendentals=0
            ),
            compiler_params=pltpu.CompilerParams(vmem_limit_bytes=grant * 1024 * 1024),
        )(*args)

    return run


def survey(transfer, edge, right, coupling):
    n = transfer.shape[0]
    (grown,), (edge_sq,), (right_sq,), (coupling_sq,) = (
        banded_dots([x], x) for x in (transfer, edge, right, coupling)
    )
    edge_trace = right_trace = jnp.zeros((1, 1), f32)
    for c in range(0, n, LANES):
        diagonal = lax.broadcasted_iota(jnp.int32, (LANES, LANES), 0) == lax.broadcasted_iota(
            jnp.int32, (LANES, LANES), 1
        )
        at = slice(c, c + LANES)
        edge_trace += total(jnp.where(diagonal, edge[at, at].astype(f32), 0.0))
        right_trace += total(jnp.where(diagonal, right[at, at].astype(f32), 0.0))
    values = (
        grown / n,
        jnp.sqrt(edge_sq / n) * jnp.sqrt(right_sq / n),
        coupling_sq / n,
        edge_trace / n * (right_trace / n),
    )
    return in_lanes(0, values)


def prepare_kernel(
    place, transfer, theta, edge, right, coupling,
    transfer_out, field_out, right_out, stats, found, bundle_far, edge_far, lifted_far,
    bundle, edge_out, lifted, sems,
):
    n = theta.shape[0]
    sizes = (place[1], place[2])
    moves = [
        pltpu.make_async_copy(*pair, sems.at[i])
        for i, pair in enumerate(((bundle, bundle_far), (edge_out, edge_far), (lifted, lifted_far)))
    ]
    for c in range(0, n, STEP):
        at = slice(c, c + STEP)
        kept = jnp.where(live(c, STEP, n, sizes), theta[at, :].astype(f32), 0.0).astype(bf16)
        field_out[at, :] = kept
        bundle[n + c : n + c + STEP, :] = kept
        bundle[at, :] = coupling[at, :]
    moves[0].start()
    for source, out in ((edge, edge_out), (right, right_out)):
        for c in range(0, n, STEP):
            turned = source[:, c : c + STEP].astype(f32).T
            out[c : c + STEP, :] = (0.5 * (source[c : c + STEP, :].astype(f32) + turned)).astype(
                out.dtype
            )
    moves[1].start()
    for c in range(0, n, STEP):
        lifted[c : c + STEP, :] = wide_dot(field_out[c : c + STEP, :], right_out[...]).astype(bf16)
    moves[2].start()
    transfer_out[...] = transfer[...]
    stats[...] = in_lanes(0, banded_dots([field_out], field_out))
    found[...] = survey(transfer, edge, right, coupling)
    for move in moves:
        move.wait()


def spread_kernel(found, after, out):
    out[...] = jnp.broadcast_to(found[...], out.shape)


def lane_entry(row, i):
    lane = lax.broadcasted_iota(jnp.int32, (1, LANES), 1)
    return jnp.sum(jnp.where(lane == i, row, 0.0), axis=1, keepdims=True)


def tuning(place, found):
    row = jnp.sum(found[...], axis=0, keepdims=True) / found.shape[0]
    grown, size, coupling_sq, trace = (lane_entry(row, i) for i in range(4))
    segment = (place[3] * ROW + place[4]).astype(f32)
    growth = jnp.exp(jnp.clip(segment * jnp.log(jnp.maximum(grown, 1e-30)), -30.0, 30.0))
    scale = size * growth + 2.0 * jnp.sqrt(coupling_sq) + 1e-12
    return in_lanes(0, (SHIFT * trace * growth, 1.0 / scale, scale))


def couple_kernel(place, coupling, bundle, below, near, far, image_far, image, sem):
    n = coupling.shape[0]
    odd = place[0] == 1

    def write(own, turned):
        own[...] = coupling[...]
        for c in range(0, n, STEP):
            turned[c : c + STEP, :] = bundle[:n, c : c + STEP].astype(f32).T.astype(bf16)
        for c in range(0, n, STEP):
            at = slice(c, c + STEP)
            image[at, :] = wide_dot(own[at, :], below[...]) + wide_dot(turned[at, :], bundle[n:, :])

    @pl.when(odd)
    def _():
        write(near, far)

    @pl.when(jnp.logical_not(odd))
    def _():
        write(far, near)

    move = pltpu.make_async_copy(image, image_far, sem)
    move.start()
    move.wait()


def identity_rows(start, rows, cols):
    row = lax.broadcasted_iota(jnp.int32, (rows, cols), 0) + start
    col = lax.broadcasted_iota(jnp.int32, (rows, cols), 1)
    return jnp.where(row == col, 1.0, 0.0)


def pair_kernel(place, own, got, high, low):
    n = own.shape[0]

    def write(first, second):
        for c in range(0, n, STEP):
            at = slice(c, c + STEP)
            product = wide_dot(first[at, :], second[...]) - identity_rows(c, STEP, n)
            high[at, :], low[at, :] = split(product)

    @pl.when(lax.rem(place[4], 2) == 0)
    def _():
        write(own, got)

    @pl.when(lax.rem(place[4], 2) == 1)
    def _():
        write(got, own)


def chain(first, second, c):
    at = slice(c, c + STEP)
    out = sum(x[at, :].astype(f32) for x in first) + sum(x[at, :].astype(f32) for x in second)
    for x in first:
        for y in second:
            out = out + wide_dot(x[at, :], y[...])
    return out


def join_kernel(which, place, own_high, own_low, got, *rest):
    n = got.shape[0]
    outs = rest[-2:] if which == 4 else rest[-1:]
    own = (own_high, own_low)
    leads = place[4] < ROW // 2 if which == 4 else lax.rem(place[3], 2) == 0

    def write(first, second):
        for c in range(0, n, STEP):
            at = slice(c, c + STEP)
            for out, part in zip(outs, split(chain(first, second, c)), strict=False):
                out[at, :] = part

    @pl.when(leads)
    def _():
        write(own, (got,))

    @pl.when(jnp.logical_not(leads))
    def _():
        write((got,), own)


def row_prefix_kernel(place, transfer_got, pair_got, high, low):
    y = place[4]
    n = transfer_got.shape[0]

    @pl.when(y == 0)
    def _():
        high[...] = jnp.zeros((n, n), bf16)
        low[...] = jnp.zeros((n, n), bf16)

    @pl.when(y == 2)
    def _():
        high[...] = pair_got[...]
        low[...] = jnp.zeros((n, n), bf16)

    @pl.when(y == 1)
    def _():
        for c in range(0, n, STEP):
            at = slice(c, c + STEP)
            alone = transfer_got[at, :].astype(f32) - identity_rows(c, STEP, n)
            high[at, :], low[at, :] = split(alone)

    @pl.when(y == 3)
    def _():
        for c in range(0, n, STEP):
            at = slice(c, c + STEP)
            alone = transfer_got[at, :].astype(f32) - identity_rows(c, STEP, n)
            high[at, :], low[at, :] = split(alone + wide_dot(pair_got[at, :], transfer_got[...]))


def segment_prefix_kernel(
    place, whole_got, row_high, row_low, high_far, low_far, high, low, sems
):
    n = whole_got.shape[0]

    @pl.when(lax.rem(place[3], 2) == 0)
    def _():
        high[...] = row_high[...]
        low[...] = row_low[...]

    @pl.when(lax.rem(place[3], 2) == 1)
    def _():
        for c in range(0, n, STEP):
            at = slice(c, c + STEP)
            high[at, :], low[at, :] = split(chain((whole_got,), (row_high, row_low), c))

    moves = [
        pltpu.make_async_copy(high, high_far, sems.at[0]),
        pltpu.make_async_copy(low, low_far, sems.at[1]),
    ]
    for move in moves:
        move.start()
    for move in moves:
        move.wait()


def segment_kernel(
    place, ahead, found, field, high_far, low_far, edge_far, couplings_far, lifted_far,
    left, left_out, next_field, tune,
    high, low, edge, couplings, lifted, prefix, turned, turned_wide, sems,
):
    sizes = (place[1], place[2])
    n = ahead.shape[0]
    pairs = (
        (high_far, high), (low_far, low), (edge_far, edge),
        (lifted_far, lifted), (couplings_far, couplings),
    )
    moves = [pltpu.make_async_copy(*pair, sems.at[i]) for i, pair in enumerate(pairs)]
    for move in moves:
        move.start()
    tuned = tuning(place, found)
    tune[...] = tuned
    shift, gain = lane_entry(tuned, 0), lane_entry(tuned, 1)
    moves[0].wait()
    moves[1].wait()

    @pl.when(place[3] < ROW // 2)
    def _():
        prefix[...] = high[...]

    @pl.when(place[3] >= ROW // 2)
    def _():
        for c in range(0, n, STEP):
            prefix[c : c + STEP, :] = chain((ahead,), (high, low), c).astype(bf16)

    moves[2].wait()
    for c in range(0, n, STEP):
        at = slice(c, c + STEP)
        value = edge[at, :] + wide_dot(edge[at, :].astype(bf16), prefix[...])
        turned_wide[at, :] = value
        turned[at, :] = value.astype(bf16)
    for c in range(0, n, STEP):
        at = slice(c, c + STEP)
        block = turned_wide[at, :] + left_transposed_dot(prefix[:, at], turned[...])
        left[at, :] = block.astype(bf16)
        left_out[at, :] = block.astype(bf16)
    moves[3].wait()
    moves[4].wait()
    for c in range(0, n, STEP):
        at = slice(c, c + STEP)
        image = wide_dot(left[at, :], lifted[...]) + couplings[at, :]
        moved = (image - shift * field[at, :].astype(f32)) * gain
        next_field[at, :] = jnp.where(live(c, STEP, n, sizes), moved, 0.0).astype(bf16)


def local_kernel(count, left, right, *rest):
    fields, (partial, stats) = rest[:count], rest[count:]
    field = fields[-1]
    n = field.shape[0]
    for c in range(0, n, STEP):
        at = slice(c, c + STEP)
        middle = wide_dot(left[at, :], field[...]).astype(bf16)
        partial[at, :] = wide_dot(middle, right[...])
    k = count - 1
    stats[...] = in_lanes(k * (k + 1) // 2, banded_dots(list(fields), field))


def near_last_kernel(near, field_a, partial, last, out):
    n = near.shape[0]
    inner = jnp.zeros((1, 1), f32)
    for c in range(0, n, STEP):
        at = slice(c, c + STEP)
        image = partial[at, :] + wide_dot(near[at, :], field_a[...])
        inner += total(image * last[at, :].astype(f32))
    k = DAVIDSON + 1
    out[...] = in_lanes(k * (k + 1) // 2, [inner])


def far_kernel(partial, far, field_b, out):
    n = far.shape[0]
    for c in range(0, n, STEP):
        at = slice(c, c + STEP)
        out[at, :] = partial[at, :] + wide_dot(far[at, :], field_b[...])


def advance_kernel(place, tune, partial, near, field_a, field, next_field):
    sizes = (place[1], place[2])
    n = field.shape[0]
    shift, gain = lane_entry(tune[...], 0), lane_entry(tune[...], 1)
    for c in range(0, n, STEP):
        at = slice(c, c + STEP)
        image = partial[at, :] + wide_dot(near[at, :], field_a[...])
        moved = (image - shift * field[at, :].astype(f32)) * gain
        next_field[at, :] = jnp.where(live(c, STEP, n, sizes), moved, 0.0).astype(bf16)


def advance_last_kernel(place, tune, partial, near, field_a, field, next_field, sent, kept):
    advance_kernel(place, tune, partial, near, field_a, field, next_field)
    half = field.shape[1] // 2

    @pl.when(place[0] == 1)
    def _():
        sent[...] = next_field[:, :half]
        kept[...] = next_field[:, half:]

    @pl.when(place[0] != 1)
    def _():
        sent[...] = next_field[:, half:]
        kept[...] = next_field[:, :half]


def close_kernel(far, got, kept, *rest):
    stats_in, out = rest[:-1], rest[-1]
    n = far.shape[0]
    inner = jnp.zeros((1, 1), f32)
    for c in range(0, n, STEP):
        at = slice(c, c + STEP)
        inner += total(wide_dot(far[at, :], got[...]) * kept[at, :].astype(f32))
    k = DAVIDSON + 1
    sums = in_lanes(k * (k + 1) // 2, [2.0 * inner])
    for piece in stats_in:
        sums += piece[...]
    out[...] = jnp.broadcast_to(sums, out.shape)


def solve_kernel(tune, sums, *rest):
    size = DAVIDSON + 1
    fields, (vector, last_energy, first_energy) = rest[:size], rest[size:]
    shift, scale = lane_entry(tune[...], 0), lane_entry(tune[...], 2)
    row = jnp.sum(sums[...], axis=0, keepdims=True)
    entry = functools.partial(lane_entry, row)
    gram = {}
    for k in range(size):
        for j in range(k + 1):
            gram[j, k] = gram[k, j] = entry(k * (k + 1) // 2 + j)
    image_gram = {}
    for j in range(size):
        for k in range(j, size):
            if j < size - 1:
                value = scale * gram[j + 1, k] + shift * gram[j, k]
            else:
                value = entry(size * (size + 1) // 2)
            image_gram[j, k] = image_gram[k, j] = value

    def form(table, a, b):
        out = jnp.zeros((1, 1), f32)
        for j, aj in enumerate(a):
            if aj is None:
                continue
            inner = jnp.zeros((1, 1), f32)
            for k, bk in enumerate(b):
                if bk is not None:
                    inner = inner + table[j, k] * bk
            out = out + aj * inner
        return out

    weights = [1.0 / jnp.sqrt(gram[0, 0] + epsilon)] + [None] * (size - 1)
    energy = first = form(image_gram, weights, weights)
    for step in range(DAVIDSON):
        turn = [None] * size
        for k in range(step + 2):
            value = None
            if weights[k] is not None:
                value = (shift - energy) * weights[k]
            if k > 0 and weights[k - 1] is not None:
                carried = scale * weights[k - 1]
                value = carried if value is None else value + carried
            turn[k] = value
        corr_norm = jnp.maximum(form(gram, turn, turn), 0.0)
        cross_term = form(image_gram, weights, turn)
        curv_term = form(image_gram, turn, turn)
        scale_norm = jnp.sqrt(corr_norm + epsilon)
        offdiag = cross_term / scale_norm
        diag_value = curv_term / (corr_norm + epsilon)
        half_gap = (diag_value - energy) / 2
        lowest = (energy + diag_value) / 2 - jnp.sqrt(half_gap * half_gap + offdiag * offdiag)
        rotation = lowest - energy
        radius = jnp.sqrt(offdiag * offdiag + rotation * rotation + epsilon)
        keep, add = offdiag / radius, rotation / scale_norm / radius
        weights = [
            None
            if t is None
            else add * t if w is None else keep * w + add * t
            for w, t in zip(weights, turn, strict=True)
        ]
        energy = lowest
    last_energy[0] = energy[0, 0]
    first_energy[0] = first[0, 0]
    n = vector.shape[0]

    def band(i, carry):
        at = pl.ds(pl.multiple_of(i * BAND, BAND), BAND)
        out = weights[0] * fields[0][at, :].astype(f32)
        for w, field in zip(weights[1:], fields[1:], strict=True):
            out = out + w * field[at, :].astype(f32)
        vector[at, :] = out
        return carry

    lax.fori_loop(0, n // BAND, band, 0)


def on_device(theta, left_edge, transfer, right_env, coupling, left_sizes, right_sizes):
    n = theta.shape[-1]
    theta, left_edge = theta[0, 0], left_edge[0]
    transfer, right_env, coupling = transfer[0, 0], right_env[0, 0], coupling[0, 0]
    seg, op = lax.axis_index("seg"), lax.axis_index("op")
    segments, sectors = lax.axis_size("seg"), lax.axis_size("op")
    y_pair = [(s, s ^ 1) for s in range(segments)]
    y_turn = [(s, s - s % ROW + ROW - 1 - s % ROW) for s in range(segments)]
    x_pair = [(s, s ^ ROW) for s in range(segments)]
    x_turn = [(s, s % ROW + ROW * (ROW - 1 - s // ROW)) for s in range(segments // 2)]
    near_swap = [(i, i ^ 1) for i in range(sectors)]
    far_swap = [(i, i + 1 if i % 2 else i - 1) for i in range(1, sectors - 1)]
    down = [(i + 1, i) for i in range(sectors - 1)]
    up = [(i, i + 1) for i in range(sectors - 1)]
    square, wide = jax.ShapeDtypeStruct((n, n), bf16), jax.ShapeDtypeStruct((n, n), f32)
    tall, double = (jax.ShapeDtypeStruct(d, bf16) for d in ((n, n // 2), (2 * n, n)))
    lanes = jax.ShapeDtypeStruct((1, LANES), f32)
    spread = jax.ShapeDtypeStruct((sectors, LANES), f32)
    number = jax.ShapeDtypeStruct((1,), f32)
    buffer = lambda rows, cols, kind=bf16: pltpu.VMEM((rows, cols), kind)
    place = jnp.stack([op % 2, left_sizes[0], right_sizes[0], seg // ROW, seg % ROW])

    def seg_send(x, route):
        return lax.ppermute(x, "seg", route)

    def op_send(x, route):
        return lax.ppermute(x, "op", route)

    def op_sum(x):
        return lax.all_to_all(x[:, None], "op", 0, 0)[:, 0]

    transfer_got = seg_send(transfer, y_pair)
    held, field, right, stats, found, bundle, edge_sym, lifted = call(
        prepare_kernel,
        (square, square, square, lanes, lanes, double, wide, square),
        out_specs=(VMEM,) * 5 + (HBM,) * 3,
        grant=GRANT,
        scratch=[buffer(2 * n, n), buffer(n, n, f32), buffer(n, n), DMA((3,))],
    )(place, transfer, theta, left_edge, right_env, coupling)
    bundle_got = op_send(bundle, down)
    below = op_send(field, up)

    pair_high, pair_low = call(pair_kernel, (square, square))(place, held, transfer_got)
    pair_got = seg_send(pair_high, y_turn)
    near, far, couplings = call(
        couple_kernel,
        (square, square, wide),
        out_specs=(VMEM, VMEM, HBM),
        grant=GRANT,
        scratch=[buffer(n, n, f32), DMA],
    )(
        place, coupling, bundle_got, below
    )
    whole_high, whole_low = call(functools.partial(join_kernel, 4), (square, square))(
        place, pair_high, pair_low, pair_got
    )
    whole_got = seg_send(whole_high, x_pair)
    row_high, row_low = call(row_prefix_kernel, (square, square))(place, transfer_got, pair_got)
    (double_high,) = call(functools.partial(join_kernel, 3), (square,), loose=2)(
        place, whole_high, whole_low, whole_got, near, row_high
    )
    ahead = seg_send(double_high, x_turn)
    high, low = call(
        segment_prefix_kernel,
        (square, square),
        out_specs=(HBM, HBM),
        grant=GRANT,
        scratch=[buffer(n, n), buffer(n, n), DMA((2,))],
    )(place, whole_got, row_high, row_low)
    found = call(spread_kernel, spread, smem=0, loose=1)(found, double_high)
    left, left_out, following, tune = call(
        segment_kernel,
        (square, square, square, lanes),
        far=5,
        grant=GRANT,
        scratch=[
            *[buffer(n, n)] * 2, *[buffer(n, n, f32)] * 2, *[buffer(n, n)] * 3,
            buffer(n, n, f32), DMA((5,)),
        ],
    )(place, ahead, op_sum(found), field, high, low, edge_sym, couplings, lifted)
    fields, pieces = [field, following], [stats]
    sent = kept = None
    for k in range(1, DAVIDSON + 1):
        last = k == DAVIDSON
        newest = fields[-1]
        field_a = op_send(newest, near_swap)
        field_b = op_send(sent if last else newest, far_swap)
        partial, stats = call(functools.partial(local_kernel, k + 1), (wide, lanes), smem=0)(
            left, right, *fields
        )
        pieces.append(stats)
        if last:
            pieces.append(call(near_last_kernel, lanes, smem=0)(near, field_a, partial, newest))
            sums = call(close_kernel, spread, smem=0)(far, field_b, kept, *pieces)
            break
        partial = call(far_kernel, wide, smem=0)(partial, far, field_b)
        if k == DAVIDSON - 1:
            following, sent, kept = call(advance_last_kernel, (square, tall, tall))(
                place, tune, partial, near, field_a, newest
            )
        else:
            following = call(advance_kernel, square)(place, tune, partial, near, field_a, newest)
        fields.append(following)
    sums = op_sum(sums)
    vector, energy, first = call(
        solve_kernel, (wide, number, number), smem=0, out_specs=(VMEM, SMEM, SMEM)
    )(tune, sums, *fields)
    return vector[None, None], left_out[None, None], energy, first


def solution(mesh):
    placed = (
        P("seg", "op", None, None),
        P("op", None, None),
        P("seg", "op", None, None),
        P("seg", "op", None, None),
        P("seg", "op", None, None),
        P("op"),
        P("op"),
    )
    return jax.shard_map(
        on_device,
        mesh=mesh,
        in_specs=placed,
        out_specs=(P("seg", "op", None, None), P("seg", "op", None, None), P("seg"), P("seg")),
        check_vma=False,
    )
```

```python
import functools

import jax
import jax.numpy as jnp
from jax import lax
from jax.experimental import pallas as pl
from jax.experimental.pallas import tpu as pltpu
from jax.sharding import PartitionSpec as P

DAVIDSON = 4
ROW = 4
LANES = 128
STEP = 256
BAND = 32
DAMP = 2.0**-14
PEAK = 32
GRANT = 52
epsilon = 1e-06

f32, bf16 = jnp.float32, jnp.bfloat16
VMEM = pl.BlockSpec(memory_space=pltpu.VMEM)
SMEM = pl.BlockSpec(memory_space=pltpu.SMEM)
LOOSE = pl.BlockSpec(memory_space=pl.ANY)
HBM = pl.BlockSpec(memory_space=pltpu.HBM)
DMA = pltpu.SemaphoreType.DMA


def wide_dot(a, b):
    return jnp.dot(a, b, preferred_element_type=f32)


def left_transposed_dot(a, b):
    return lax.dot_general(a, b, (((0,), (0,)), ((), ())), preferred_element_type=f32)


def split(x):
    high = x.astype(bf16)
    return high, (x - high.astype(f32)).astype(bf16)


def total(x):
    return jnp.sum(jnp.sum(x, axis=0, keepdims=True), axis=1, keepdims=True)


def in_lanes(first, values):
    lane = lax.broadcasted_iota(jnp.int32, (1, LANES), 1)
    out = jnp.zeros((1, LANES), f32)
    for i, value in enumerate(values):
        out = jnp.where(lane == first + i, value, out)
    return out


def live(start, rows, cols, sizes):
    row = lax.broadcasted_iota(jnp.int32, (rows, cols), 0) + start
    col = lax.broadcasted_iota(jnp.int32, (rows, cols), 1)
    return (row < sizes[0]) & (col < sizes[1])


def whole(parts, at):
    return sum(p[at, :].astype(f32) for p in parts)


def over_bands(n, body, start):
    def band(i, carry):
        return body(pl.ds(pl.multiple_of(i * BAND, BAND), BAND), carry)

    return lax.fori_loop(0, n // BAND, band, start)


def gram_row(fields, peaks):
    newest = fields[-1]
    n, cols = newest[0].shape

    def fold(x):
        return x.reshape(BAND // 8, 8, cols)

    def widest(at, top):
        return jnp.maximum(top, jnp.max(fold(jnp.abs(whole(newest, at))), axis=0))

    top = over_bands(n, widest, jnp.zeros((8, cols), f32))
    peak = jnp.max(jnp.max(top, axis=0, keepdims=True), axis=1, keepdims=True)
    peak = jnp.where(peak > 0.0, peak, 1.0)
    peaks = [*peaks, peak]

    def products(at, sums):
        mine = whole(newest, at) / peak
        return tuple(
            s + jnp.sum(fold(whole(f, at) / p * mine), axis=0)
            for s, f, p in zip(sums, fields, peaks, strict=True)
        )

    sums = over_bands(n, products, tuple(jnp.zeros((8, cols), f32) for _ in fields))
    k = len(fields) - 1
    return in_lanes(k * (k + 1) // 2, [total(x) for x in sums]) + in_lanes(PEAK + k, [peak])


def call(kernel, out, smem=1, loose=0, far=0, scratch=(), out_specs=None, grant=20):
    def run(*args):
        return pl.pallas_call(
            kernel,
            out_shape=out,
            in_specs=[SMEM] * smem
            + [VMEM] * (len(args) - smem - loose - far)
            + [LOOSE] * loose
            + [HBM] * far,
            out_specs=jax.tree.map(lambda _: VMEM, out) if out_specs is None else out_specs,
            scratch_shapes=list(scratch),
            cost_estimate=pl.CostEstimate(
                flops=1, bytes_accessed=1, transcendentals=0
            ),
            compiler_params=pltpu.CompilerParams(vmem_limit_bytes=grant * 1024 * 1024),
        )(*args)

    return run


def prepare_kernel(
    place, transfer, theta, edge, right, coupling,
    transfer_out, field_out, right_out, stats, bundle_far, edge_far, lifted_far,
    bundle, edge_out, lifted, sems,
):
    n = theta.shape[0]
    sizes = (place[1], place[2])
    moves = [
        pltpu.make_async_copy(*pair, sems.at[i])
        for i, pair in enumerate(((bundle, bundle_far), (edge_out, edge_far), (lifted, lifted_far)))
    ]
    for c in range(0, n, STEP):
        at = slice(c, c + STEP)
        kept = jnp.where(live(c, STEP, n, sizes), theta[at, :].astype(f32), 0.0).astype(bf16)
        field_out[at, :] = kept
        bundle[n + c : n + c + STEP, :] = kept
        bundle[at, :] = coupling[at, :]
    moves[0].start()
    for source, out in ((edge, edge_out), (right, right_out)):
        for c in range(0, n, STEP):
            turned = source[:, c : c + STEP].astype(f32).T
            out[c : c + STEP, :] = (0.5 * (source[c : c + STEP, :].astype(f32) + turned)).astype(
                out.dtype
            )
    moves[1].start()
    for c in range(0, n, STEP):
        parts = split(wide_dot(field_out[c : c + STEP, :], right_out[...]))
        for i, part in enumerate(parts):
            lifted[i * n + c : i * n + c + STEP, :] = part
    moves[2].start()
    transfer_out[...] = transfer[...]
    stats[...] = gram_row([(field_out,)], [])
    for move in moves:
        move.wait()


def lane_entry(row, i):
    lane = lax.broadcasted_iota(jnp.int32, row.shape, 1)
    return jnp.sum(jnp.where(lane == i, row, 0.0), axis=1, keepdims=True)


def couple_kernel(place, coupling, bundle, below, near, far, image_far, image, sem):
    n = coupling.shape[0]
    odd = place[0] == 1

    def write(own, turned):
        own[...] = coupling[...]
        for c in range(0, n, STEP):
            turned[c : c + STEP, :] = bundle[:n, c : c + STEP].astype(f32).T.astype(bf16)
        for c in range(0, n, STEP):
            at = slice(c, c + STEP)
            image[at, :] = wide_dot(own[at, :], below[...]) + wide_dot(turned[at, :], bundle[n:, :])

    @pl.when(odd)
    def _():
        write(near, far)

    @pl.when(jnp.logical_not(odd))
    def _():
        write(far, near)

    move = pltpu.make_async_copy(image, image_far, sem)
    move.start()
    move.wait()


def identity_rows(start, rows, cols):
    row = lax.broadcasted_iota(jnp.int32, (rows, cols), 0) + start
    col = lax.broadcasted_iota(jnp.int32, (rows, cols), 1)
    return jnp.where(row == col, 1.0, 0.0)


def pair_kernel(place, own, got, high, low):
    n = own.shape[0]

    def write(first, second):
        for c in range(0, n, STEP):
            at = slice(c, c + STEP)
            product = wide_dot(first[at, :], second[...]) - identity_rows(c, STEP, n)
            high[at, :], low[at, :] = split(product)

    @pl.when(lax.rem(place[4], 2) == 0)
    def _():
        write(own, got)

    @pl.when(lax.rem(place[4], 2) == 1)
    def _():
        write(got, own)


def chain(first, second, c):
    at = slice(c, c + STEP)
    out = sum(x[at, :].astype(f32) for x in first) + sum(x[at, :].astype(f32) for x in second)
    for x in first:
        for y in second:
            out = out + wide_dot(x[at, :], y[...])
    return out


def join_kernel(which, place, own_high, own_low, got, *rest):
    n = got.shape[0]
    outs = rest[-2:] if which == 4 else rest[-1:]
    own = (own_high, own_low)
    leads = place[4] < ROW // 2 if which == 4 else lax.rem(place[3], 2) == 0

    def write(first, second):
        for c in range(0, n, STEP):
            at = slice(c, c + STEP)
            for out, part in zip(outs, split(chain(first, second, c)), strict=False):
                out[at, :] = part

    @pl.when(leads)
    def _():
        write(own, (got,))

    @pl.when(jnp.logical_not(leads))
    def _():
        write((got,), own)


def row_prefix_kernel(place, transfer_got, pair_got, high, low):
    y = place[4]
    n = transfer_got.shape[0]

    @pl.when(y == 0)
    def _():
        high[...] = jnp.zeros((n, n), bf16)
        low[...] = jnp.zeros((n, n), bf16)

    @pl.when(y == 2)
    def _():
        high[...] = pair_got[...]
        low[...] = jnp.zeros((n, n), bf16)

    @pl.when(y == 1)
    def _():
        for c in range(0, n, STEP):
            at = slice(c, c + STEP)
            alone = transfer_got[at, :].astype(f32) - identity_rows(c, STEP, n)
            high[at, :], low[at, :] = split(alone)

    @pl.when(y == 3)
    def _():
        for c in range(0, n, STEP):
            at = slice(c, c + STEP)
            alone = transfer_got[at, :].astype(f32) - identity_rows(c, STEP, n)
            high[at, :], low[at, :] = split(alone + wide_dot(pair_got[at, :], transfer_got[...]))


def segment_prefix_kernel(
    place, whole_got, row_high, row_low, high_far, low_far, high, low, sems
):
    n = whole_got.shape[0]

    @pl.when(lax.rem(place[3], 2) == 0)
    def _():
        high[...] = row_high[...]
        low[...] = row_low[...]

    @pl.when(lax.rem(place[3], 2) == 1)
    def _():
        for c in range(0, n, STEP):
            at = slice(c, c + STEP)
            high[at, :], low[at, :] = split(chain((whole_got,), (row_high, row_low), c))

    moves = [
        pltpu.make_async_copy(high, high_far, sems.at[0]),
        pltpu.make_async_copy(low, low_far, sems.at[1]),
    ]
    for move in moves:
        move.start()
    for move in moves:
        move.wait()


def segment_kernel(
    place, ahead, high_far, low_far, edge_far, couplings_far, lifted_far,
    left, left_out, next_high, next_low,
    high, low, edge, couplings, lifted, prefix, turned, turned_wide, sems,
):
    sizes = (place[1], place[2])
    n = ahead.shape[0]
    pairs = (
        (high_far, high), (low_far, low), (edge_far, edge),
        (lifted_far, lifted), (couplings_far, couplings),
    )
    moves = [pltpu.make_async_copy(*pair, sems.at[i]) for i, pair in enumerate(pairs)]
    for move in moves:
        move.start()
    moves[0].wait()
    moves[1].wait()

    @pl.when(place[3] < ROW // 2)
    def _():
        prefix[...] = high[...]

    @pl.when(place[3] >= ROW // 2)
    def _():
        for c in range(0, n, STEP):
            prefix[c : c + STEP, :] = chain((ahead,), (high, low), c).astype(bf16)

    moves[2].wait()
    for c in range(0, n, STEP):
        at = slice(c, c + STEP)
        value = edge[at, :] + wide_dot(edge[at, :].astype(bf16), prefix[...])
        turned_wide[at, :] = value
        turned[at, :] = value.astype(bf16)
    for c in range(0, n, STEP):
        at = slice(c, c + STEP)
        block = turned_wide[at, :] + left_transposed_dot(prefix[:, at], turned[...])
        left[at, :] = block.astype(bf16)
        left_out[at, :] = block.astype(bf16)
    moves[3].wait()
    moves[4].wait()
    for c in range(0, n, STEP):
        at = slice(c, c + STEP)
        image = wide_dot(left[at, :], lifted[:n, :]) + wide_dot(left[at, :], lifted[n:, :])
        image = jnp.where(live(c, STEP, n, sizes), image + couplings[at, :], 0.0)
        next_high[at, :], next_low[at, :] = split(DAMP * image)


def local_kernel(count, stats_in, left, right, *rest):
    parts, (partial, stats) = rest[: 2 * count - 1], rest[2 * count - 1 :]
    fields = [parts[:1]] + [parts[i : i + 2] for i in range(1, 2 * count - 1, 2)]
    newest = fields[-1]
    n = left.shape[0]
    for c in range(0, n, STEP):
        at = slice(c, c + STEP)
        middle = sum(wide_dot(left[at, :], x[...]) for x in newest)
        partial[at, :] = sum(wide_dot(x, right[...]) for x in split(middle))
    before = stats_in[...]
    peaks = [lane_entry(before, PEAK + k) for k in range(count - 1)]
    stats[...] = before + gram_row(fields, peaks)


def far_kernel(partial, far, field_b, out):
    n = far.shape[0]
    for c in range(0, n, STEP):
        at = slice(c, c + STEP)
        out[at, :] = partial[at, :] + wide_dot(far[at, :], field_b[...])


def advance_kernel(place, partial, near, field_a, next_high, next_low, *halves):
    sizes = (place[1], place[2])
    n = near.shape[0]
    for c in range(0, n, STEP):
        at = slice(c, c + STEP)
        image = partial[at, :] + wide_dot(near[at, :], field_a[...])
        image = jnp.where(live(c, STEP, n, sizes), image, 0.0)
        next_high[at, :], next_low[at, :] = split(DAMP * image)
    if not halves:
        return
    sent, kept = halves
    half = n // 2

    @pl.when(place[0] == 1)
    def _():
        sent[...] = next_high[:, :half]
        kept[...] = next_high[:, half:].astype(f32) + next_low[:, half:].astype(f32)

    @pl.when(place[0] != 1)
    def _():
        sent[...] = next_high[:, half:]
        kept[...] = next_high[:, :half].astype(f32) + next_low[:, :half].astype(f32)


def far_last_kernel(stats_in, far, got, kept, out):
    n = far.shape[0]
    peak = lane_entry(stats_in[...], PEAK + DAVIDSON)
    inner = jnp.zeros((1, 1), f32)
    for c in range(0, n, STEP):
        at = slice(c, c + STEP)
        inner += total(wide_dot(far[at, :], got[...]) / peak * (kept[at, :] / peak))
    k = DAVIDSON + 1
    out[...] = stats_in[...] + in_lanes(k * (k + 1) // 2, [2.0 * inner])


def close_kernel(stats_in, near, field_a, partial, high, low, out):
    n = near.shape[0]
    peak = lane_entry(stats_in[...], PEAK + DAVIDSON)
    inner = jnp.zeros((1, 1), f32)
    for c in range(0, n, STEP):
        at = slice(c, c + STEP)
        image = partial[at, :] + wide_dot(near[at, :], field_a[...])
        inner += total(image / peak * (whole((high, low), at) / peak))
    k = DAVIDSON + 1
    out[...] = jnp.broadcast_to(
        stats_in[...] + in_lanes(k * (k + 1) // 2, [inner]), out.shape
    )


def solve_kernel(sums, *rest):
    size = DAVIDSON + 1
    parts, (vector, last_energy, first_energy) = rest[: 2 * size - 1], rest[2 * size - 1 :]
    fields = [parts[:1]] + [parts[i : i + 2] for i in range(1, 2 * size - 1, 2)]
    table = sums[...]
    local_peaks = [lane_entry(table, PEAK + k) for k in range(size)]
    peaks = [jnp.max(p, axis=0, keepdims=True) for p in local_peaks]
    ratios = [p / top for p, top in zip(local_peaks, peaks, strict=True)]
    scales = [peaks[k + 1] / peaks[k] * (1.0 / DAMP) for k in range(size - 1)]

    def entry(i, j, k):
        return jnp.sum(lane_entry(table, i) * ratios[j] * ratios[k], axis=0, keepdims=True)

    gram = {}
    for k in range(size):
        for j in range(k + 1):
            gram[j, k] = gram[k, j] = entry(k * (k + 1) // 2 + j, j, k)
    image_gram = {}
    for j in range(size):
        for k in range(j, size):
            if j < size - 1:
                value = scales[j] * gram[j + 1, k]
            else:
                value = entry(size * (size + 1) // 2, j, j)
            image_gram[j, k] = image_gram[k, j] = value

    def form(table, a, b):
        out = jnp.zeros((1, 1), f32)
        for j, aj in enumerate(a):
            if aj is None:
                continue
            inner = jnp.zeros((1, 1), f32)
            for k, bk in enumerate(b):
                if bk is not None:
                    inner = inner + table[j, k] * bk
            out = out + aj * inner
        return out

    start_norm = jnp.sqrt(peaks[0] * peaks[0] * gram[0, 0] + epsilon)
    weights = [peaks[0] / start_norm] + [None] * (size - 1)
    energy = first = form(image_gram, weights, weights)
    for step in range(DAVIDSON):
        turn = [None] * size
        for k in range(step + 2):
            value = None
            if weights[k] is not None:
                value = -energy * weights[k]
            if k > 0 and weights[k - 1] is not None:
                carried = scales[k - 1] * weights[k - 1]
                value = carried if value is None else value + carried
            turn[k] = value
        corr_norm = jnp.maximum(form(gram, turn, turn), 0.0)
        cross_term = form(image_gram, weights, turn)
        curv_term = form(image_gram, turn, turn)
        scale_norm = jnp.sqrt(corr_norm + epsilon)
        offdiag = cross_term / scale_norm
        diag_value = curv_term / (corr_norm + epsilon)
        half_gap = (diag_value - energy) / 2
        lowest = (energy + diag_value) / 2 - jnp.sqrt(half_gap * half_gap + offdiag * offdiag)
        rotation = lowest - energy
        radius = jnp.sqrt(offdiag * offdiag + rotation * rotation + epsilon)
        keep, add = offdiag / radius, rotation / scale_norm / radius
        weights = [
            None
            if t is None
            else add * t if w is None else keep * w + add * t
            for w, t in zip(weights, turn, strict=True)
        ]
        energy = lowest
    last_energy[0] = energy[0, 0]
    first_energy[0] = first[0, 0]
    weights = [w / p for w, p in zip(weights, peaks, strict=True)]

    def band(at, carry):
        vector[at, :] = sum(
            w * whole(field, at) for w, field in zip(weights, fields, strict=True)
        )
        return carry

    over_bands(vector.shape[0], band, 0)


def on_device(theta, left_edge, transfer, right_env, coupling, left_sizes, right_sizes):
    n = theta.shape[-1]
    theta, left_edge = theta[0, 0], left_edge[0]
    transfer, right_env, coupling = transfer[0, 0], right_env[0, 0], coupling[0, 0]
    seg, op = lax.axis_index("seg"), lax.axis_index("op")
    segments, sectors = lax.axis_size("seg"), lax.axis_size("op")
    y_pair = [(s, s ^ 1) for s in range(segments)]
    y_turn = [(s, s - s % ROW + ROW - 1 - s % ROW) for s in range(segments)]
    x_pair = [(s, s ^ ROW) for s in range(segments)]
    x_turn = [(s, s % ROW + ROW * (ROW - 1 - s // ROW)) for s in range(segments // 2)]
    near_swap = [(i, i ^ 1) for i in range(sectors)]
    far_swap = [(i, i + 1 if i % 2 else i - 1) for i in range(1, sectors - 1)]
    down = [(i + 1, i) for i in range(sectors - 1)]
    up = [(i, i + 1) for i in range(sectors - 1)]
    square, wide = jax.ShapeDtypeStruct((n, n), bf16), jax.ShapeDtypeStruct((n, n), f32)
    tall, double = (jax.ShapeDtypeStruct(d, bf16) for d in ((n, n // 2), (2 * n, n)))
    tall_wide = jax.ShapeDtypeStruct((n, n // 2), f32)
    lanes = jax.ShapeDtypeStruct((1, LANES), f32)
    spread = jax.ShapeDtypeStruct((sectors, LANES), f32)
    number = jax.ShapeDtypeStruct((1,), f32)
    buffer = lambda rows, cols, kind=bf16: pltpu.VMEM((rows, cols), kind)
    place = jnp.stack([op % 2, left_sizes[0], right_sizes[0], seg // ROW, seg % ROW])

    def seg_send(x, route):
        return lax.ppermute(x, "seg", route)

    def op_send(x, route):
        return lax.ppermute(x, "op", route)

    def op_sum(x):
        return lax.all_to_all(x[:, None], "op", 0, 0)[:, 0]

    transfer_got = seg_send(transfer, y_pair)
    held, field, right, stats, bundle, edge_sym, lifted = call(
        prepare_kernel,
        (square, square, square, lanes, double, wide, double),
        out_specs=(VMEM,) * 4 + (HBM,) * 3,
        grant=GRANT,
        scratch=[buffer(2 * n, n), buffer(n, n, f32), buffer(2 * n, n), DMA((3,))],
    )(place, transfer, theta, left_edge, right_env, coupling)
    bundle_got = op_send(bundle, down)
    below = op_send(field, up)

    pair_high, pair_low = call(pair_kernel, (square, square))(place, held, transfer_got)
    pair_got = seg_send(pair_high, y_turn)
    near, far, couplings = call(
        couple_kernel,
        (square, square, wide),
        out_specs=(VMEM, VMEM, HBM),
        grant=GRANT,
        scratch=[buffer(n, n, f32), DMA],
    )(
        place, coupling, bundle_got, below
    )
    whole_high, whole_low = call(functools.partial(join_kernel, 4), (square, square))(
        place, pair_high, pair_low, pair_got
    )
    whole_got = seg_send(whole_high, x_pair)
    row_high, row_low = call(row_prefix_kernel, (square, square))(place, transfer_got, pair_got)
    (double_high,) = call(functools.partial(join_kernel, 3), (square,), loose=2)(
        place, whole_high, whole_low, whole_got, near, row_high
    )
    ahead = seg_send(double_high, x_turn)
    high, low = call(
        segment_prefix_kernel,
        (square, square),
        out_specs=(HBM, HBM),
        grant=GRANT,
        scratch=[buffer(n, n), buffer(n, n), DMA((2,))],
    )(place, whole_got, row_high, row_low)
    left, left_out, *following = call(
        segment_kernel,
        (square, square, square, square),
        far=5,
        grant=GRANT,
        scratch=[
            *[buffer(n, n)] * 2, *[buffer(n, n, f32)] * 2, buffer(2 * n, n), *[buffer(n, n)] * 2,
            buffer(n, n, f32), DMA((5,)),
        ],
    )(place, ahead, high, low, edge_sym, couplings, lifted)
    fields = [(field,), tuple(following)]
    for k in range(1, DAVIDSON + 1):
        high, low = fields[-1]
        last = k == DAVIDSON
        field_a = op_send(high, near_swap)
        field_b = op_send(sent if last else high, far_swap)
        partial, stats = call(functools.partial(local_kernel, k + 1), (wide, lanes), smem=0)(
            stats, left, right, *sum(fields, ())
        )
        if last:
            stats = call(far_last_kernel, lanes, smem=0)(stats, far, field_b, kept)
            sums = call(close_kernel, spread, smem=0)(stats, near, field_a, partial, high, low)
            break
        partial = call(far_kernel, wide, smem=0)(partial, far, field_b)
        if k == DAVIDSON - 1:
            *following, sent, kept = call(advance_kernel, (square, square, tall, tall_wide))(
                place, partial, near, field_a
            )
        else:
            following = call(advance_kernel, (square, square))(place, partial, near, field_a)
        fields.append(tuple(following))
    sums = op_sum(sums)
    vector, energy, first = call(
        solve_kernel, (wide, number, number), smem=0, out_specs=(VMEM, SMEM, SMEM)
    )(sums, *sum(fields, ()))
    return vector[None, None], left_out[None, None], energy, first


def solution(mesh):
    placed = (
        P("seg", "op", None, None),
        P("op", None, None),
        P("seg", "op", None, None),
        P("seg", "op", None, None),
        P("seg", "op", None, None),
        P("op"),
        P("op"),
    )
    return jax.shard_map(
        on_device,
        mesh=mesh,
        in_specs=placed,
        out_specs=(P("seg", "op", None, None), P("seg", "op", None, None), P("seg"), P("seg")),
        check_vma=False,
    )
```

```python
import functools

import jax
import jax.numpy as jnp
from jax import lax
from jax.experimental import pallas as pl
from jax.experimental.pallas import tpu as pltpu
from jax.sharding import PartitionSpec as P

DAVIDSON = 4
ROW = 4
LANES = 128
STEP = 256
BAND = 32
DAMP = 2.0**-14
PEAK = 32
GRANT = 51
epsilon = 1e-06

f32, bf16 = jnp.float32, jnp.bfloat16
VMEM = pl.BlockSpec(memory_space=pltpu.VMEM)
SMEM = pl.BlockSpec(memory_space=pltpu.SMEM)
LOOSE = pl.BlockSpec(memory_space=pl.ANY)
HBM = pl.BlockSpec(memory_space=pltpu.HBM)
DMA = pltpu.SemaphoreType.DMA


def wide_dot(a, b):
    return jnp.dot(a, b, preferred_element_type=f32)


def left_transposed_dot(a, b):
    return lax.dot_general(a, b, (((0,), (0,)), ((), ())), preferred_element_type=f32)


def split(x):
    high = x.astype(bf16)
    return high, (x - high.astype(f32)).astype(bf16)


def total(x):
    return jnp.sum(jnp.sum(x, axis=0, keepdims=True), axis=1, keepdims=True)


def in_lanes(first, values):
    lane = lax.broadcasted_iota(jnp.int32, (1, LANES), 1)
    out = jnp.zeros((1, LANES), f32)
    for i, value in enumerate(values):
        out = jnp.where(lane == first + i, value, out)
    return out


def live(start, rows, cols, sizes):
    row = lax.broadcasted_iota(jnp.int32, (rows, cols), 0) + start
    col = lax.broadcasted_iota(jnp.int32, (rows, cols), 1)
    return (row < sizes[0]) & (col < sizes[1])


def whole(parts, at):
    return sum(p[at, :].astype(f32) for p in parts)


def over_bands(n, body, start):
    def band(i, carry):
        return body(pl.ds(pl.multiple_of(i * BAND, BAND), BAND), carry)

    return lax.fori_loop(0, n // BAND, band, start)


def gram_row(fields, peaks):
    newest = fields[-1]
    n, cols = newest[0].shape

    def fold(x):
        return x.reshape(BAND // 8, 8, cols)

    def widest(at, top):
        return jnp.maximum(top, jnp.max(fold(jnp.abs(whole(newest, at))), axis=0))

    top = over_bands(n, widest, jnp.zeros((8, cols), f32))
    peak = jnp.max(jnp.max(top, axis=0, keepdims=True), axis=1, keepdims=True)
    peak = jnp.where(peak > 0.0, peak, 1.0)
    inverse = 1.0 / peak

    def products(at, sums):
        mine = whole(newest, at) * inverse
        others = [whole(f, at) for f in fields[:-1]]
        return tuple(
            s + jnp.sum(fold(x * mine), axis=0) for s, x in zip(sums, [*others, mine], strict=True)
        )

    sums = over_bands(n, products, tuple(jnp.zeros((8, cols), f32) for _ in fields))
    k = len(fields) - 1
    values = [total(x) / p for x, p in zip(sums[:-1], peaks, strict=True)] + [total(sums[-1])]
    return in_lanes(k * (k + 1) // 2, values) + in_lanes(PEAK + k, [peak])


def call(kernel, out, smem=1, loose=0, far=0, scratch=(), out_specs=None, grant=20):
    def run(*args):
        return pl.pallas_call(
            kernel,
            out_shape=out,
            in_specs=[SMEM] * smem
            + [VMEM] * (len(args) - smem - loose - far)
            + [LOOSE] * loose
            + [HBM] * far,
            out_specs=jax.tree.map(lambda _: VMEM, out) if out_specs is None else out_specs,
            scratch_shapes=list(scratch),
            cost_estimate=pl.CostEstimate(
                flops=1, bytes_accessed=1, transcendentals=0
            ),
            compiler_params=pltpu.CompilerParams(vmem_limit_bytes=grant * 1024 * 1024),
        )(*args)

    return run


def prepare_kernel(
    place, transfer, theta, edge, right, coupling,
    transfer_out, field_out, right_out, stats, bundle_far, edge_far, lifted_far,
    bundle, edge_out, lifted, sems,
):
    n = theta.shape[0]
    sizes = (place[1], place[2])
    moves = [
        pltpu.make_async_copy(*pair, sems.at[i])
        for i, pair in enumerate(((bundle, bundle_far), (edge_out, edge_far), (lifted, lifted_far)))
    ]
    for c in range(0, n, STEP):
        at = slice(c, c + STEP)
        kept = jnp.where(live(c, STEP, n, sizes), theta[at, :].astype(f32), 0.0).astype(bf16)
        field_out[at, :] = kept
        bundle[n + c : n + c + STEP, :] = kept
        bundle[at, :] = coupling[at, :]
    moves[0].start()
    for source, out in ((edge, edge_out), (right, right_out)):
        for c in range(0, n, STEP):
            turned = source[:, c : c + STEP].astype(f32).T
            out[c : c + STEP, :] = (0.5 * (source[c : c + STEP, :].astype(f32) + turned)).astype(
                out.dtype
            )
    moves[1].start()
    for c in range(0, n, STEP):
        parts = split(wide_dot(field_out[c : c + STEP, :], right_out[...]))
        for i, part in enumerate(parts):
            lifted[i * n + c : i * n + c + STEP, :] = part
    moves[2].start()
    transfer_out[...] = transfer[...]
    stats[...] = gram_row([(field_out,)], [])
    for move in moves:
        move.wait()


def lane_entry(row, i):
    lane = lax.broadcasted_iota(jnp.int32, row.shape, 1)
    return jnp.sum(jnp.where(lane == i, row, 0.0), axis=1, keepdims=True)


def couple_kernel(place, coupling, bundle, below, near, far, image_far, image, sem):
    n = coupling.shape[0]
    odd = place[0] == 1

    def write(own, turned):
        own[...] = coupling[...]
        for c in range(0, n, STEP):
            turned[c : c + STEP, :] = bundle[:n, c : c + STEP].astype(f32).T.astype(bf16)
        for c in range(0, n, STEP):
            at = slice(c, c + STEP)
            image[at, :] = wide_dot(own[at, :], below[...]) + wide_dot(turned[at, :], bundle[n:, :])

    @pl.when(odd)
    def _():
        write(near, far)

    @pl.when(jnp.logical_not(odd))
    def _():
        write(far, near)

    move = pltpu.make_async_copy(image, image_far, sem)
    move.start()
    move.wait()


def identity_rows(start, rows, cols):
    row = lax.broadcasted_iota(jnp.int32, (rows, cols), 0) + start
    col = lax.broadcasted_iota(jnp.int32, (rows, cols), 1)
    return jnp.where(row == col, 1.0, 0.0)


def pair_kernel(place, own, got, high, low):
    n = own.shape[0]

    def write(first, second):
        for c in range(0, n, STEP):
            at = slice(c, c + STEP)
            product = wide_dot(first[at, :], second[...]) - identity_rows(c, STEP, n)
            high[at, :], low[at, :] = split(product)

    @pl.when(lax.rem(place[4], 2) == 0)
    def _():
        write(own, got)

    @pl.when(lax.rem(place[4], 2) == 1)
    def _():
        write(got, own)


def chain(first, second, c):
    at = slice(c, c + STEP)
    out = sum(x[at, :].astype(f32) for x in first) + sum(x[at, :].astype(f32) for x in second)
    for x in first:
        for y in second:
            out = out + wide_dot(x[at, :], y[...])
    return out


def join_kernel(which, place, own_high, own_low, got, *rest):
    n = got.shape[0]
    outs = rest[-2:] if which == 4 else rest[-1:]
    own = (own_high, own_low)
    leads = place[4] < ROW // 2 if which == 4 else lax.rem(place[3], 2) == 0

    def write(first, second):
        for c in range(0, n, STEP):
            at = slice(c, c + STEP)
            for out, part in zip(outs, split(chain(first, second, c)), strict=False):
                out[at, :] = part

    @pl.when(leads)
    def _():
        write(own, (got,))

    @pl.when(jnp.logical_not(leads))
    def _():
        write((got,), own)


def row_prefix_kernel(place, transfer_got, pair_got, high, low):
    y = place[4]
    n = transfer_got.shape[0]

    @pl.when(y == 0)
    def _():
        high[...] = jnp.zeros((n, n), bf16)
        low[...] = jnp.zeros((n, n), bf16)

    @pl.when(y == 2)
    def _():
        high[...] = pair_got[...]
        low[...] = jnp.zeros((n, n), bf16)

    @pl.when(y == 1)
    def _():
        for c in range(0, n, STEP):
            at = slice(c, c + STEP)
            alone = transfer_got[at, :].astype(f32) - identity_rows(c, STEP, n)
            high[at, :], low[at, :] = split(alone)

    @pl.when(y == 3)
    def _():
        for c in range(0, n, STEP):
            at = slice(c, c + STEP)
            alone = transfer_got[at, :].astype(f32) - identity_rows(c, STEP, n)
            high[at, :], low[at, :] = split(alone + wide_dot(pair_got[at, :], transfer_got[...]))


def segment_prefix_kernel(
    place, whole_got, row_high, row_low, high_far, high, sem
):
    n = whole_got.shape[0]

    @pl.when(lax.rem(place[3], 2) == 0)
    def _():
        high[...] = row_high[...]

    @pl.when(lax.rem(place[3], 2) == 1)
    def _():
        for c in range(0, n, STEP):
            at = slice(c, c + STEP)
            high[at, :] = chain((whole_got,), (row_high, row_low), c).astype(bf16)

    move = pltpu.make_async_copy(high, high_far, sem)
    move.start()
    move.wait()


def segment_kernel(
    place, ahead, high_far, edge_far, couplings_far, lifted_far,
    left, left_out, next_high, next_low,
    high, edge, couplings, lifted, prefix, turned, turned_wide, sems,
):
    sizes = (place[1], place[2])
    n = ahead.shape[0]
    pairs = ((high_far, high), (edge_far, edge), (lifted_far, lifted), (couplings_far, couplings))
    moves = [pltpu.make_async_copy(*pair, sems.at[i]) for i, pair in enumerate(pairs)]
    for move in moves:
        move.start()
    moves[0].wait()

    @pl.when(place[3] < ROW // 2)
    def _():
        prefix[...] = high[...]

    @pl.when(place[3] >= ROW // 2)
    def _():
        for c in range(0, n, STEP):
            prefix[c : c + STEP, :] = chain((ahead,), (high,), c).astype(bf16)

    moves[1].wait()
    for c in range(0, n, STEP):
        at = slice(c, c + STEP)
        value = edge[at, :] + wide_dot(edge[at, :].astype(bf16), prefix[...])
        turned_wide[at, :] = value
        turned[at, :] = value.astype(bf16)
    for c in range(0, n, STEP):
        at = slice(c, c + STEP)
        block = turned_wide[at, :] + left_transposed_dot(prefix[:, at], turned[...])
        left[at, :] = block.astype(bf16)
        left_out[at, :] = block.astype(bf16)
    moves[2].wait()
    moves[3].wait()
    for c in range(0, n, STEP):
        at = slice(c, c + STEP)
        image = wide_dot(left[at, :], lifted[:n, :]) + wide_dot(left[at, :], lifted[n:, :])
        image = jnp.where(live(c, STEP, n, sizes), image + couplings[at, :], 0.0)
        next_high[at, :], next_low[at, :] = split(DAMP * image)


def local_kernel(count, stats_in, left, right, *rest):
    parts, (partial, stats) = rest[: 2 * count - 1], rest[2 * count - 1 :]
    fields = [parts[:1]] + [parts[i : i + 2] for i in range(1, 2 * count - 1, 2)]
    newest = fields[-1]
    n = left.shape[0]
    for c in range(0, n, STEP):
        at = slice(c, c + STEP)
        middle = sum(wide_dot(left[at, :], x[...]) for x in newest)
        partial[at, :] = sum(wide_dot(x, right[...]) for x in split(middle))
    before = stats_in[...]
    peaks = [lane_entry(before, PEAK + k) for k in range(count - 1)]
    stats[...] = before + gram_row(fields, peaks)


def far_kernel(partial, far, field_b, out):
    n = far.shape[0]
    for c in range(0, n, STEP):
        at = slice(c, c + STEP)
        out[at, :] = partial[at, :] + wide_dot(far[at, :], field_b[...])


def advance_kernel(place, partial, near, field_a, next_high, next_low, *halves):
    sizes = (place[1], place[2])
    n = near.shape[0]
    for c in range(0, n, STEP):
        at = slice(c, c + STEP)
        image = partial[at, :] + wide_dot(near[at, :], field_a[...])
        image = jnp.where(live(c, STEP, n, sizes), image, 0.0)
        next_high[at, :], next_low[at, :] = split(DAMP * image)
    if not halves:
        return
    sent, kept = halves
    half = n // 2

    @pl.when(place[0] == 1)
    def _():
        sent[...] = next_high[:, :half]
        kept[...] = next_high[:, half:].astype(f32) + next_low[:, half:].astype(f32)

    @pl.when(place[0] != 1)
    def _():
        sent[...] = next_high[:, half:]
        kept[...] = next_high[:, :half].astype(f32) + next_low[:, :half].astype(f32)


def crossing(matrix, got, kept, inverse):
    inner = jnp.zeros((1, 1), f32)
    for c in range(0, matrix.shape[0], STEP):
        at = slice(c, c + STEP)
        inner += total(wide_dot(matrix[at, :], got[...]) * inverse * (kept[at, :] * inverse))
    return 2.0 * inner


def far_last_kernel(stats_in, far, got, kept, out):
    inverse = 1.0 / lane_entry(stats_in[...], PEAK + DAVIDSON)
    k = DAVIDSON + 1
    out[...] = stats_in[...] + in_lanes(k * (k + 1) // 2, [crossing(far, got, kept, inverse)])


def close_kernel(stats_in, near, got, kept, partial, high, low, out):
    inverse = 1.0 / lane_entry(stats_in[...], PEAK + DAVIDSON)
    inner = crossing(near, got, kept, inverse)
    for c in range(0, near.shape[0], STEP):
        at = slice(c, c + STEP)
        inner += total(partial[at, :] * inverse * (whole((high, low), at) * inverse))
    k = DAVIDSON + 1
    sums = stats_in[...] + in_lanes(k * (k + 1) // 2, [inner])
    out[...] = jnp.broadcast_to(sums, out.shape)


def solve_kernel(sums, *rest):
    size = DAVIDSON + 1
    parts, (vector, last_energy, first_energy) = rest[: 2 * size - 1], rest[2 * size - 1 :]
    fields = [parts[:1]] + [parts[i : i + 2] for i in range(1, 2 * size - 1, 2)]
    table = sums[...]
    local_peaks = [lane_entry(table, PEAK + k) for k in range(size)]
    peaks = [jnp.max(p, axis=0, keepdims=True) for p in local_peaks]
    ratios = [p / top for p, top in zip(local_peaks, peaks, strict=True)]
    scales = [peaks[k + 1] / peaks[k] * (1.0 / DAMP) for k in range(size - 1)]

    def entry(i, j, k):
        return jnp.sum(lane_entry(table, i) * ratios[j] * ratios[k], axis=0, keepdims=True)

    gram = {}
    for k in range(size):
        for j in range(k + 1):
            gram[j, k] = gram[k, j] = entry(k * (k + 1) // 2 + j, j, k)
    image_gram = {}
    for j in range(size):
        for k in range(j, size):
            if j < size - 1:
                value = scales[j] * gram[j + 1, k]
            else:
                value = entry(size * (size + 1) // 2, j, j)
            image_gram[j, k] = image_gram[k, j] = value

    def form(table, a, b):
        out = jnp.zeros((1, 1), f32)
        for j, aj in enumerate(a):
            if aj is None:
                continue
            inner = jnp.zeros((1, 1), f32)
            for k, bk in enumerate(b):
                if bk is not None:
                    inner = inner + table[j, k] * bk
            out = out + aj * inner
        return out

    start_norm = jnp.sqrt(peaks[0] * peaks[0] * gram[0, 0] + epsilon)
    weights = [peaks[0] / start_norm] + [None] * (size - 1)
    energy = first = form(image_gram, weights, weights)
    for step in range(DAVIDSON):
        turn = [None] * size
        for k in range(step + 2):
            value = None
            if weights[k] is not None:
                value = -energy * weights[k]
            if k > 0 and weights[k - 1] is not None:
                carried = scales[k - 1] * weights[k - 1]
                value = carried if value is None else value + carried
            turn[k] = value
        corr_norm = jnp.maximum(form(gram, turn, turn), 0.0)
        cross_term = form(image_gram, weights, turn)
        curv_term = form(image_gram, turn, turn)
        scale_norm = jnp.sqrt(corr_norm + epsilon)
        offdiag = cross_term / scale_norm
        diag_value = curv_term / (corr_norm + epsilon)
        half_gap = (diag_value - energy) / 2
        lowest = (energy + diag_value) / 2 - jnp.sqrt(half_gap * half_gap + offdiag * offdiag)
        rotation = lowest - energy
        radius = jnp.sqrt(offdiag * offdiag + rotation * rotation + epsilon)
        keep, add = offdiag / radius, rotation / scale_norm / radius
        weights = [
            None
            if t is None
            else add * t if w is None else keep * w + add * t
            for w, t in zip(weights, turn, strict=True)
        ]
        energy = lowest
    last_energy[0] = energy[0, 0]
    first_energy[0] = first[0, 0]
    weights = [w / p for w, p in zip(weights, peaks, strict=True)]

    def band(at, carry):
        vector[at, :] = sum(
            w * whole(field, at) for w, field in zip(weights, fields, strict=True)
        )
        return carry

    over_bands(vector.shape[0], band, 0)


def on_device(theta, left_edge, transfer, right_env, coupling, left_sizes, right_sizes):
    n = theta.shape[-1]
    theta, left_edge = theta[0, 0], left_edge[0]
    transfer, right_env, coupling = transfer[0, 0], right_env[0, 0], coupling[0, 0]
    seg, op = lax.axis_index("seg"), lax.axis_index("op")
    segments, sectors = lax.axis_size("seg"), lax.axis_size("op")
    y_pair = [(s, s ^ 1) for s in range(segments)]
    y_turn = [(s, s - s % ROW + ROW - 1 - s % ROW) for s in range(segments)]
    x_pair = [(s, s ^ ROW) for s in range(segments)]
    x_turn = [(s, s % ROW + ROW * (ROW - 1 - s // ROW)) for s in range(segments // 2)]
    near_swap = [(i, i ^ 1) for i in range(sectors)]
    far_swap = [(i, i + 1 if i % 2 else i - 1) for i in range(1, sectors - 1)]
    down = [(i + 1, i) for i in range(sectors - 1)]
    up = [(i, i + 1) for i in range(sectors - 1)]
    square, wide = jax.ShapeDtypeStruct((n, n), bf16), jax.ShapeDtypeStruct((n, n), f32)
    tall, double = (jax.ShapeDtypeStruct(d, bf16) for d in ((n, n // 2), (2 * n, n)))
    tall_wide = jax.ShapeDtypeStruct((n, n // 2), f32)
    lanes = jax.ShapeDtypeStruct((1, LANES), f32)
    spread = jax.ShapeDtypeStruct((sectors, LANES), f32)
    number = jax.ShapeDtypeStruct((1,), f32)
    buffer = lambda rows, cols, kind=bf16: pltpu.VMEM((rows, cols), kind)
    place = jnp.stack([op % 2, left_sizes[0], right_sizes[0], seg // ROW, seg % ROW])

    def seg_send(x, route):
        return lax.ppermute(x, "seg", route)

    def op_send(x, route):
        return lax.ppermute(x, "op", route)

    def op_sum(x):
        return lax.all_to_all(x[:, None], "op", 0, 0)[:, 0]

    transfer_got = seg_send(transfer, y_pair)
    held, field, right, stats, bundle, edge_sym, lifted = call(
        prepare_kernel,
        (square, square, square, lanes, double, wide, double),
        out_specs=(VMEM,) * 4 + (HBM,) * 3,
        grant=GRANT,
        scratch=[buffer(2 * n, n), buffer(n, n, f32), buffer(2 * n, n), DMA((3,))],
    )(place, transfer, theta, left_edge, right_env, coupling)
    bundle_got = op_send(bundle, down)
    below = op_send(field, up)

    pair_high, pair_low = call(pair_kernel, (square, square))(place, held, transfer_got)
    pair_got = seg_send(pair_high, y_turn)
    near, far, couplings = call(
        couple_kernel,
        (square, square, wide),
        out_specs=(VMEM, VMEM, HBM),
        grant=GRANT,
        scratch=[buffer(n, n, f32), DMA],
    )(
        place, coupling, bundle_got, below
    )
    whole_high, whole_low = call(functools.partial(join_kernel, 4), (square, square))(
        place, pair_high, pair_low, pair_got
    )
    whole_got = seg_send(whole_high, x_pair)
    row_high, row_low = call(row_prefix_kernel, (square, square))(place, transfer_got, pair_got)
    (double_high,) = call(functools.partial(join_kernel, 3), (square,), loose=2)(
        place, whole_high, whole_low, whole_got, near, row_high
    )
    ahead = seg_send(double_high, x_turn)
    high = call(
        segment_prefix_kernel,
        square,
        out_specs=HBM,
        grant=GRANT,
        scratch=[buffer(n, n), DMA],
    )(place, whole_got, row_high, row_low)
    left, left_out, *following = call(
        segment_kernel,
        (square, square, square, square),
        far=4,
        grant=GRANT,
        scratch=[
            buffer(n, n), *[buffer(n, n, f32)] * 2, buffer(2 * n, n), *[buffer(n, n)] * 2,
            buffer(n, n, f32), DMA((4,)),
        ],
    )(place, ahead, high, edge_sym, couplings, lifted)
    fields = [(field,), tuple(following)]
    for k in range(1, DAVIDSON + 1):
        high, low = fields[-1]
        last = k == DAVIDSON
        field_a = op_send(sent if last else high, near_swap)
        field_b = op_send(sent if last else high, far_swap)
        partial, stats = call(functools.partial(local_kernel, k + 1), (wide, lanes), smem=0)(
            stats, left, right, *sum(fields, ())
        )
        if last:
            stats = call(far_last_kernel, lanes, smem=0)(stats, far, field_b, kept)
            sums = call(close_kernel, spread, smem=0)(
                stats, near, field_a, kept, partial, high, low
            )
            break
        partial = call(far_kernel, wide, smem=0)(partial, far, field_b)
        if k == DAVIDSON - 1:
            *following, sent, kept = call(advance_kernel, (square, square, tall, tall_wide))(
                place, partial, near, field_a
            )
        else:
            following = call(advance_kernel, (square, square))(place, partial, near, field_a)
        fields.append(tuple(following))
    sums = op_sum(sums)
    vector, energy, first = call(
        solve_kernel, (wide, number, number), smem=0, out_specs=(VMEM, SMEM, SMEM)
    )(sums, *sum(fields, ()))
    return vector[None, None], left_out[None, None], energy, first


def solution(mesh):
    placed = (
        P("seg", "op", None, None),
        P("op", None, None),
        P("seg", "op", None, None),
        P("seg", "op", None, None),
        P("seg", "op", None, None),
        P("op"),
        P("op"),
    )
    return jax.shard_map(
        on_device,
        mesh=mesh,
        in_specs=placed,
        out_specs=(P("seg", "op", None, None), P("seg", "op", None, None), P("seg"), P("seg")),
        check_vma=False,
    )
```

```python
import functools

import jax
import jax.numpy as jnp
from jax import lax
from jax.experimental import pallas as pl
from jax.experimental.pallas import tpu as pltpu
from jax.sharding import PartitionSpec as P

DAVIDSON = 4
ROW = 4
LANES = 128
STEP = 256
BAND = 32
DAMP = 2.0**-14
PEAK = 32
GRANT = 51
epsilon = 1e-06

f32, bf16 = jnp.float32, jnp.bfloat16
VMEM = pl.BlockSpec(memory_space=pltpu.VMEM)
SMEM = pl.BlockSpec(memory_space=pltpu.SMEM)
LOOSE = pl.BlockSpec(memory_space=pl.ANY)
HBM = pl.BlockSpec(memory_space=pltpu.HBM)
DMA = pltpu.SemaphoreType.DMA


def wide_dot(a, b):
    return jnp.dot(a, b, preferred_element_type=f32)


def left_transposed_dot(a, b):
    return lax.dot_general(a, b, (((0,), (0,)), ((), ())), preferred_element_type=f32)


def split(x):
    high = x.astype(bf16)
    return high, (x - high.astype(f32)).astype(bf16)


def total(x):
    return jnp.sum(jnp.sum(x, axis=0, keepdims=True), axis=1, keepdims=True)


def in_lanes(first, values):
    lane = lax.broadcasted_iota(jnp.int32, (1, LANES), 1)
    out = jnp.zeros((1, LANES), f32)
    for i, value in enumerate(values):
        out = jnp.where(lane == first + i, value, out)
    return out


def live(start, rows, cols, sizes):
    row = lax.broadcasted_iota(jnp.int32, (rows, cols), 0) + start
    col = lax.broadcasted_iota(jnp.int32, (rows, cols), 1)
    return (row < sizes[0]) & (col < sizes[1])


def whole(parts, at):
    return sum(p[at, :].astype(f32) for p in parts)


def over_bands(n, body, start):
    def band(i, carry):
        return body(pl.ds(pl.multiple_of(i * BAND, BAND), BAND), carry)

    return lax.fori_loop(0, n // BAND, band, start)


def gram_row(fields, peaks):
    newest = fields[-1]
    n, cols = newest[0].shape

    def fold(x):
        return x.reshape(BAND // 8, 8, cols)

    def widest(at, top):
        return jnp.maximum(top, jnp.max(fold(jnp.abs(whole(newest, at))), axis=0))

    top = over_bands(n, widest, jnp.zeros((8, cols), f32))
    peak = jnp.max(jnp.max(top, axis=0, keepdims=True), axis=1, keepdims=True)
    peak = jnp.where(peak > 0.0, peak, 1.0)
    inverse = 1.0 / peak

    def products(at, sums):
        mine = whole(newest, at) * inverse
        others = [whole(f, at) for f in fields[:-1]]
        return tuple(
            s + jnp.sum(fold(x * mine), axis=0) for s, x in zip(sums, [*others, mine], strict=True)
        )

    sums = over_bands(n, products, tuple(jnp.zeros((8, cols), f32) for _ in fields))
    k = len(fields) - 1
    values = [total(x) / p for x, p in zip(sums[:-1], peaks, strict=True)] + [total(sums[-1])]
    return in_lanes(k * (k + 1) // 2, values) + in_lanes(PEAK + k, [peak])


def call(kernel, out, smem=1, loose=0, far=0, scratch=(), out_specs=None, grant=20):
    def run(*args):
        return pl.pallas_call(
            kernel,
            out_shape=out,
            in_specs=[SMEM] * smem
            + [VMEM] * (len(args) - smem - loose - far)
            + [LOOSE] * loose
            + [HBM] * far,
            out_specs=jax.tree.map(lambda _: VMEM, out) if out_specs is None else out_specs,
            scratch_shapes=list(scratch),
            cost_estimate=pl.CostEstimate(
                flops=1, bytes_accessed=1, transcendentals=0
            ),
            compiler_params=pltpu.CompilerParams(vmem_limit_bytes=grant * 1024 * 1024),
        )(*args)

    return run


def prepare_kernel(
    place, transfer, theta, edge, right, coupling,
    transfer_out, field_out, right_out, stats, bundle_far, edge_far, lifted_far,
    bundle, edge_out, lifted, sems,
):
    n = theta.shape[0]
    sizes = (place[1], place[2])
    moves = [
        pltpu.make_async_copy(*pair, sems.at[i])
        for i, pair in enumerate(((bundle, bundle_far), (edge_out, edge_far), (lifted, lifted_far)))
    ]
    for c in range(0, n, STEP):
        at = slice(c, c + STEP)
        kept = jnp.where(live(c, STEP, n, sizes), theta[at, :].astype(f32), 0.0).astype(bf16)
        field_out[at, :] = kept
        bundle[n + c : n + c + STEP, :] = kept
        bundle[at, :] = coupling[at, :]
    moves[0].start()
    for source, out in ((edge, edge_out), (right, right_out)):
        for c in range(0, n, STEP):
            turned = source[:, c : c + STEP].astype(f32).T
            out[c : c + STEP, :] = (0.5 * (source[c : c + STEP, :].astype(f32) + turned)).astype(
                out.dtype
            )
    moves[1].start()
    for c in range(0, n, STEP):
        parts = split(wide_dot(field_out[c : c + STEP, :], right_out[...]))
        for i, part in enumerate(parts):
            lifted[i * n + c : i * n + c + STEP, :] = part
    moves[2].start()
    transfer_out[...] = transfer[...]
    stats[...] = gram_row([(field_out,)], [])
    for move in moves:
        move.wait()


def lane_entry(row, i):
    lane = lax.broadcasted_iota(jnp.int32, row.shape, 1)
    return jnp.sum(jnp.where(lane == i, row, 0.0), axis=1, keepdims=True)


def couple_kernel(place, coupling, bundle, below, near, far, image_far, image, sem):
    n = coupling.shape[0]
    odd = place[0] == 1

    def write(own, turned):
        own[...] = coupling[...]
        for c in range(0, n, STEP):
            turned[c : c + STEP, :] = bundle[:n, c : c + STEP].astype(f32).T.astype(bf16)
        for c in range(0, n, STEP):
            at = slice(c, c + STEP)
            image[at, :] = wide_dot(own[at, :], below[...]) + wide_dot(turned[at, :], bundle[n:, :])

    @pl.when(odd)
    def _():
        write(near, far)

    @pl.when(jnp.logical_not(odd))
    def _():
        write(far, near)

    move = pltpu.make_async_copy(image, image_far, sem)
    move.start()
    move.wait()


def identity_rows(start, rows, cols):
    row = lax.broadcasted_iota(jnp.int32, (rows, cols), 0) + start
    col = lax.broadcasted_iota(jnp.int32, (rows, cols), 1)
    return jnp.where(row == col, 1.0, 0.0)


def pair_kernel(place, own, got, high, low):
    n = own.shape[0]

    def write(first, second):
        for c in range(0, n, STEP):
            at = slice(c, c + STEP)
            product = wide_dot(first[at, :], second[...]) - identity_rows(c, STEP, n)
            high[at, :], low[at, :] = split(product)

    @pl.when(lax.rem(place[4], 2) == 0)
    def _():
        write(own, got)

    @pl.when(lax.rem(place[4], 2) == 1)
    def _():
        write(got, own)


def chain(first, second, c):
    at = slice(c, c + STEP)
    out = sum(x[at, :].astype(f32) for x in first) + sum(x[at, :].astype(f32) for x in second)
    for x in first:
        for y in second:
            out = out + wide_dot(x[at, :], y[...])
    return out


def join_kernel(which, place, own_high, own_low, got, *rest):
    n = got.shape[0]
    outs = rest[-2:] if which == 4 else rest[-1:]
    own = (own_high, own_low)
    leads = place[4] < ROW // 2 if which == 4 else lax.rem(place[3], 2) == 0

    def write(first, second):
        for c in range(0, n, STEP):
            at = slice(c, c + STEP)
            for out, part in zip(outs, split(chain(first, second, c)), strict=False):
                out[at, :] = part

    @pl.when(leads)
    def _():
        write(own, (got,))

    @pl.when(jnp.logical_not(leads))
    def _():
        write((got,), own)


def row_prefix_kernel(place, transfer_got, pair_got, high, low):
    y = place[4]
    n = transfer_got.shape[0]

    @pl.when(y == 0)
    def _():
        high[...] = jnp.zeros((n, n), bf16)
        low[...] = jnp.zeros((n, n), bf16)

    @pl.when(y == 2)
    def _():
        high[...] = pair_got[...]
        low[...] = jnp.zeros((n, n), bf16)

    @pl.when(y == 1)
    def _():
        for c in range(0, n, STEP):
            at = slice(c, c + STEP)
            alone = transfer_got[at, :].astype(f32) - identity_rows(c, STEP, n)
            high[at, :], low[at, :] = split(alone)

    @pl.when(y == 3)
    def _():
        for c in range(0, n, STEP):
            at = slice(c, c + STEP)
            alone = transfer_got[at, :].astype(f32) - identity_rows(c, STEP, n)
            high[at, :], low[at, :] = split(alone + wide_dot(pair_got[at, :], transfer_got[...]))


def segment_prefix_kernel(
    place, whole_got, row_high, row_low, high_far, high, sem
):
    n = whole_got.shape[0]

    @pl.when(lax.rem(place[3], 2) == 0)
    def _():
        high[...] = row_high[...]

    @pl.when(lax.rem(place[3], 2) == 1)
    def _():
        for c in range(0, n, STEP):
            at = slice(c, c + STEP)
            high[at, :] = chain((whole_got,), (row_high, row_low), c).astype(bf16)

    move = pltpu.make_async_copy(high, high_far, sem)
    move.start()
    move.wait()


def segment_kernel(
    place, ahead, high_far, edge_far, couplings_far, lifted_far,
    left, left_out, next_high, next_low,
    high, edge, couplings, lifted, prefix, turned, turned_wide, sems,
):
    sizes = (place[1], place[2])
    n = ahead.shape[0]
    pairs = ((high_far, high), (edge_far, edge), (lifted_far, lifted), (couplings_far, couplings))
    moves = [pltpu.make_async_copy(*pair, sems.at[i]) for i, pair in enumerate(pairs)]
    for move in moves:
        move.start()
    moves[0].wait()

    @pl.when(place[3] < ROW // 2)
    def _():
        prefix[...] = high[...]

    @pl.when(place[3] >= ROW // 2)
    def _():
        for c in range(0, n, STEP):
            prefix[c : c + STEP, :] = chain((ahead,), (high,), c).astype(bf16)

    moves[1].wait()
    for c in range(0, n, STEP):
        at = slice(c, c + STEP)
        value = edge[at, :] + wide_dot(edge[at, :].astype(bf16), prefix[...])
        turned_wide[at, :] = value
        turned[at, :] = value.astype(bf16)
    for c in range(0, n, STEP):
        at = slice(c, c + STEP)
        block = turned_wide[at, :] + left_transposed_dot(prefix[:, at], turned[...])
        left[at, :] = block.astype(bf16)
        left_out[at, :] = block.astype(bf16)
    moves[2].wait()
    moves[3].wait()
    for c in range(0, n, STEP):
        at = slice(c, c + STEP)
        image = wide_dot(left[at, :], lifted[:n, :]) + wide_dot(left[at, :], lifted[n:, :])
        image = jnp.where(live(c, STEP, n, sizes), image + couplings[at, :], 0.0)
        next_high[at, :], next_low[at, :] = split(DAMP * image)


def local_kernel(count, stats_in, left, right, *rest):
    parts, (partial, stats) = rest[: 2 * count - 1], rest[2 * count - 1 :]
    fields = [parts[:1]] + [parts[i : i + 2] for i in range(1, 2 * count - 1, 2)]
    newest = fields[-1]
    n = left.shape[0]
    for c in range(0, n, STEP):
        at = slice(c, c + STEP)
        middle = sum(wide_dot(left[at, :], x[...]) for x in newest)
        partial[at, :] = sum(wide_dot(x, right[...]) for x in split(middle))
    before = stats_in[...]
    peaks = [lane_entry(before, PEAK + k) for k in range(count - 1)]
    stats[...] = before + gram_row(fields, peaks)


def far_kernel(partial, far, field_b, out):
    n = far.shape[0]
    for c in range(0, n, STEP):
        at = slice(c, c + STEP)
        out[at, :] = partial[at, :] + wide_dot(far[at, :], field_b[...])


def advance_kernel(place, partial, near, field_a, next_high, next_low, *halves):
    sizes = (place[1], place[2])
    n = near.shape[0]
    for c in range(0, n, STEP):
        at = slice(c, c + STEP)
        image = partial[at, :] + wide_dot(near[at, :], field_a[...])
        image = jnp.where(live(c, STEP, n, sizes), image, 0.0)
        next_high[at, :], next_low[at, :] = split(DAMP * image)
    if not halves:
        return
    sent, kept = halves
    half = n // 2

    @pl.when(place[0] == 1)
    def _():
        sent[...] = next_high[:, :half]
        kept[...] = next_high[:, half:].astype(f32) + next_low[:, half:].astype(f32)

    @pl.when(place[0] != 1)
    def _():
        sent[...] = next_high[:, half:]
        kept[...] = next_high[:, :half].astype(f32) + next_low[:, :half].astype(f32)


def crossing(matrix, got, kept, inverse):
    inner = jnp.zeros((1, 1), f32)
    for c in range(0, matrix.shape[0], STEP):
        at = slice(c, c + STEP)
        inner += total(wide_dot(matrix[at, :], got[...]) * inverse * (kept[at, :] * inverse))
    return 2.0 * inner


def far_last_kernel(stats_in, far, got, kept, out):
    inverse = 1.0 / lane_entry(stats_in[...], PEAK + DAVIDSON)
    k = DAVIDSON + 1
    out[...] = stats_in[...] + in_lanes(k * (k + 1) // 2, [crossing(far, got, kept, inverse)])


def close_kernel(stats_in, near, got, kept, partial, high, low, out):
    inverse = 1.0 / lane_entry(stats_in[...], PEAK + DAVIDSON)
    inner = crossing(near, got, kept, inverse)
    for c in range(0, near.shape[0], STEP):
        at = slice(c, c + STEP)
        inner += total(partial[at, :] * inverse * (whole((high, low), at) * inverse))
    k = DAVIDSON + 1
    sums = stats_in[...] + in_lanes(k * (k + 1) // 2, [inner])
    out[...] = jnp.broadcast_to(sums, out.shape)


def solve_kernel(sums, *rest):
    size = DAVIDSON + 1
    parts, (vector, last_energy, first_energy) = rest[: 2 * size - 1], rest[2 * size - 1 :]
    fields = [parts[:1]] + [parts[i : i + 2] for i in range(1, 2 * size - 1, 2)]
    table = sums[...]
    local_peaks = [lane_entry(table, PEAK + k) for k in range(size)]
    peaks = [jnp.max(p, axis=0, keepdims=True) for p in local_peaks]
    ratios = [p / top for p, top in zip(local_peaks, peaks, strict=True)]
    scales = [peaks[k + 1] / peaks[k] * (1.0 / DAMP) for k in range(size - 1)]

    def entry(i, j, k):
        return jnp.sum(lane_entry(table, i) * ratios[j] * ratios[k], axis=0, keepdims=True)

    gram = {}
    for k in range(size):
        for j in range(k + 1):
            gram[j, k] = gram[k, j] = entry(k * (k + 1) // 2 + j, j, k)
    image_gram = {}
    for j in range(size):
        for k in range(j, size):
            if j < size - 1:
                value = scales[j] * gram[j + 1, k]
            else:
                value = entry(size * (size + 1) // 2, j, j)
            image_gram[j, k] = image_gram[k, j] = value

    def form(table, a, b):
        out = jnp.zeros((1, 1), f32)
        for j, aj in enumerate(a):
            if aj is None:
                continue
            inner = jnp.zeros((1, 1), f32)
            for k, bk in enumerate(b):
                if bk is not None:
                    inner = inner + table[j, k] * bk
            out = out + aj * inner
        return out

    start_norm = jnp.sqrt(peaks[0] * peaks[0] * gram[0, 0] + epsilon)
    weights = [peaks[0] / start_norm] + [None] * (size - 1)
    energy = first = form(image_gram, weights, weights)
    for step in range(DAVIDSON):
        turn = [None] * size
        for k in range(step + 2):
            value = None
            if weights[k] is not None:
                value = -energy * weights[k]
            if k > 0 and weights[k - 1] is not None:
                carried = scales[k - 1] * weights[k - 1]
                value = carried if value is None else value + carried
            turn[k] = value
        corr_norm = jnp.maximum(form(gram, turn, turn), 0.0)
        cross_term = form(image_gram, weights, turn)
        curv_term = form(image_gram, turn, turn)
        scale_norm = jnp.sqrt(corr_norm + epsilon)
        offdiag = cross_term / scale_norm
        diag_value = curv_term / (corr_norm + epsilon)
        half_gap = (diag_value - energy) / 2
        lowest = (energy + diag_value) / 2 - jnp.sqrt(half_gap * half_gap + offdiag * offdiag)
        rotation = lowest - energy
        radius = jnp.sqrt(offdiag * offdiag + rotation * rotation + epsilon)
        keep, add = offdiag / radius, rotation / scale_norm / radius
        weights = [
            None
            if t is None
            else add * t if w is None else keep * w + add * t
            for w, t in zip(weights, turn, strict=True)
        ]
        energy = lowest
    last_energy[0] = energy[0, 0]
    first_energy[0] = first[0, 0]
    weights = [w / p for w, p in zip(weights, peaks, strict=True)]

    def band(at, carry):
        vector[at, :] = sum(
            w * whole(field, at) for w, field in zip(weights, fields, strict=True)
        )
        return carry

    over_bands(vector.shape[0], band, 0)


def on_device(theta, left_edge, transfer, right_env, coupling, left_sizes, right_sizes):
    n = theta.shape[-1]
    theta, left_edge = theta[0, 0], left_edge[0]
    transfer, right_env, coupling = transfer[0, 0], right_env[0, 0], coupling[0, 0]
    seg, op = lax.axis_index("seg"), lax.axis_index("op")
    segments, sectors = lax.axis_size("seg"), lax.axis_size("op")
    y_pair = [(s, s ^ 1) for s in range(segments)]
    y_turn = [(s, s - s % ROW + ROW - 1 - s % ROW) for s in range(segments)]
    x_pair = [(s, s ^ ROW) for s in range(segments)]
    x_turn = [(s, s % ROW + ROW * (ROW - 1 - s // ROW)) for s in range(segments // 2)]
    near_swap = [(i, i ^ 1) for i in range(sectors)]
    far_swap = [(i, i + 1 if i % 2 else i - 1) for i in range(1, sectors - 1)]
    down = [(i + 1, i) for i in range(sectors - 1)]
    up = [(i, i + 1) for i in range(sectors - 1)]
    square, wide = jax.ShapeDtypeStruct((n, n), bf16), jax.ShapeDtypeStruct((n, n), f32)
    tall, double = (jax.ShapeDtypeStruct(d, bf16) for d in ((n, n // 2), (2 * n, n)))
    tall_wide = jax.ShapeDtypeStruct((n, n // 2), f32)
    lanes = jax.ShapeDtypeStruct((1, LANES), f32)
    spread = jax.ShapeDtypeStruct((sectors, LANES), f32)
    number = jax.ShapeDtypeStruct((1,), f32)
    buffer = lambda rows, cols, kind=bf16: pltpu.VMEM((rows, cols), kind)
    place = jnp.stack([op % 2, left_sizes[0], right_sizes[0], seg // ROW, seg % ROW])

    def seg_send(x, route):
        return lax.ppermute(x, "seg", route)

    def op_send(x, route):
        return lax.ppermute(x, "op", route)

    def op_sum(x):
        order = [*range(sectors // 2, sectors), *range(sectors // 2)]
        return lax.all_to_all(x[:, None], "op", 0, 0, axis_index_groups=[order])[:, 0]

    transfer_got = seg_send(transfer, y_pair)
    held, field, right, stats, bundle, edge_sym, lifted = call(
        prepare_kernel,
        (square, square, square, lanes, double, wide, double),
        out_specs=(VMEM,) * 4 + (HBM,) * 3,
        grant=GRANT,
        scratch=[buffer(2 * n, n), buffer(n, n, f32), buffer(2 * n, n), DMA((3,))],
    )(place, transfer, theta, left_edge, right_env, coupling)
    bundle_got = op_send(bundle, down)
    below = op_send(field, up)

    pair_high, pair_low = call(pair_kernel, (square, square))(place, held, transfer_got)
    pair_got = seg_send(pair_high, y_turn)
    near, far, couplings = call(
        couple_kernel,
        (square, square, wide),
        out_specs=(VMEM, VMEM, HBM),
        grant=GRANT,
        scratch=[buffer(n, n, f32), DMA],
    )(
        place, coupling, bundle_got, below
    )
    whole_high, whole_low = call(functools.partial(join_kernel, 4), (square, square))(
        place, pair_high, pair_low, pair_got
    )
    whole_got = seg_send(whole_high, x_pair)
    row_high, row_low = call(row_prefix_kernel, (square, square))(place, transfer_got, pair_got)
    (double_high,) = call(functools.partial(join_kernel, 3), (square,), loose=2)(
        place, whole_high, whole_low, whole_got, near, row_high
    )
    ahead = seg_send(double_high, x_turn)
    high = call(
        segment_prefix_kernel,
        square,
        out_specs=HBM,
        grant=GRANT,
        scratch=[buffer(n, n), DMA],
    )(place, whole_got, row_high, row_low)
    left, left_out, *following = call(
        segment_kernel,
        (square, square, square, square),
        far=4,
        grant=GRANT,
        scratch=[
            buffer(n, n), *[buffer(n, n, f32)] * 2, buffer(2 * n, n), *[buffer(n, n)] * 2,
            buffer(n, n, f32), DMA((4,)),
        ],
    )(place, ahead, high, edge_sym, couplings, lifted)
    fields = [(field,), tuple(following)]
    for k in range(1, DAVIDSON + 1):
        high, low = fields[-1]
        last = k == DAVIDSON
        field_a = op_send(sent if last else high, near_swap)
        field_b = op_send(sent if last else high, far_swap)
        partial, stats = call(functools.partial(local_kernel, k + 1), (wide, lanes), smem=0)(
            stats, left, right, *sum(fields, ())
        )
        if last:
            stats = call(far_last_kernel, lanes, smem=0)(stats, far, field_b, kept)
            sums = call(close_kernel, spread, smem=0)(
                stats, near, field_a, kept, partial, high, low
            )
            break
        partial = call(far_kernel, wide, smem=0)(partial, far, field_b)
        if k == DAVIDSON - 1:
            *following, sent, kept = call(advance_kernel, (square, square, tall, tall_wide))(
                place, partial, near, field_a
            )
        else:
            following = call(advance_kernel, (square, square))(place, partial, near, field_a)
        fields.append(tuple(following))
    sums = op_sum(sums)
    vector, energy, first = call(
        solve_kernel, (wide, number, number), smem=0, out_specs=(VMEM, SMEM, SMEM)
    )(sums, *sum(fields, ()))
    return vector[None, None], left_out[None, None], energy, first


def solution(mesh):
    placed = (
        P("seg", "op", None, None),
        P("op", None, None),
        P("seg", "op", None, None),
        P("seg", "op", None, None),
        P("seg", "op", None, None),
        P("op"),
        P("op"),
    )
    return jax.shard_map(
        on_device,
        mesh=mesh,
        in_specs=placed,
        out_specs=(P("seg", "op", None, None), P("seg", "op", None, None), P("seg"), P("seg")),
        check_vma=False,
    )
```
